32 devices in a mesh: blk: 4 (over y, x), dom: 8 (over z, core).
Axes of the slice: x: 2, y: 2, z: 4, core: 2. Of those that a mesh axis runs over, the one named last changes fastest.
Arguments:
- positions: float32 [3, 32768], P(None, ('blk', 'dom')), may hold values from -6 to 6
- line_vectors: float32 [3, 32768], P(None, ('blk', 'dom')), may hold values from -6 to 6
- burgers: float32 [3, 32768], P(None, ('blk', 'dom')), may hold values from -6 to 6
- mobility: float32 [32768], P(('blk', 'dom')), may hold values from 0.5 to 2
- close_list: int32 [32, 32768], P(None, ('blk', 'dom')), may hold values from 0 to 256, as said below
- ghost_map: int32 [4, 16384], P(None, ('blk', 'dom')), may hold values from 0 to 1023, as said below
Outputs:
- new_positions: float32 [3, 32768], P(None, ('blk', 'dom'))
- velocity: float32 [3, 32768], P(None, ('blk', 'dom'))
The draws below stay inside these ranges and needn't reach their ends.
Inputs may be any that keep to these rules, and one draw needn't show every extreme that they name: `close_list`: each entry is a place in the window of the segment's cell: below 128 a segment of the same cell, 128 + u the u-th row of the cell's ghost window, and 256 an empty slot. `ghost_map`: for each subcycle, each device's run of 512 entries holds first 256 distinct local segment numbers below 512 (the ghosts of the lower domain), the first of them 0, then 256 distinct local numbers of at least 1024 - 512 (the ghosts of the upper domain), the first of them 1024 - 1.
All inputs are finite; a program needn't handle non-finite values.
Results may differ from the reference program's by a relative error of at most 0.0005.
Values sent between devices are 32-bit elements; how exact they have to be, the bound alone decides.
No kernel may reach another device: no remote copies, remote signals or barrier semaphores. Data moves between devices by JAX's collectives and lax.ppermute only.
A program may use at most 64 MiB of HBM per device.

```python
import math
import jax
import jax.numpy as jnp
from jax import lax

CELLS = 8
CELL_SEGS = 128
SLOTS = 32
GHOSTS = 256
SUBS = 4
SEG_DEV = 1024
RIM_ROWS = 512
WINDOWS = 4
SEGS = 32768
N_BLK = 4
N_DOM = 8


def draw_close_list(key, part):
    device_count = SEGS // SEG_DEV
    empty_slot = 2 * CELL_SEGS
    fill_key, level_key, index_key = jax.random.split(key, 3)
    levels = jax.random.randint(level_key, (device_count,), 3, 10)
    level_rows = jnp.repeat(levels, SEG_DEV)
    chance = jax.random.randint(fill_key, (SLOTS, SEGS), 0, 10)
    partner = jax.random.randint(index_key, (SLOTS, SEGS), 0, empty_slot)
    return jnp.where(chance < level_rows[None, :], partner, empty_slot).astype(jnp.int32)


def draw_ghost_map(key, part):
    device_count = SEGS // SEG_DEV
    key_list = jax.random.split(key, SUBS * device_count * 2)

    def one_side(one_key):
        picked = jax.random.permutation(one_key, RIM_ROWS - 1)[:GHOSTS - 1] + 1
        return jnp.concatenate([jnp.zeros((1,), jnp.int32), picked.astype(jnp.int32)])
    side_rows = jax.vmap(one_side)(key_list).reshape(SUBS, device_count, 2, GHOSTS)
    lower_side = side_rows[:, :, 0]
    upper_side = SEG_DEV - 1 - side_rows[:, :, 1]
    return jnp.stack([lower_side, upper_side], 2).reshape(SUBS, device_count * 2 * GHOSTS).astype(jnp.int32)


def level_of(key, dims, cuts, least, largest):
    gain, own = 1.0, jax.random.fold_in(key, 6)
    for axis_at, shards_of in cuts:
        steps = jnp.exp(jax.random.uniform(jax.random.fold_in(own, axis_at), (shards_of,), jnp.float32, least / len(cuts), largest / len(cuts)))
        gain = gain * jnp.repeat(steps, dims[axis_at] // shards_of).reshape([-1 if axis == axis_at else 1 for axis in range(len(dims))])
    return gain


def centred(key, extent, spread, limit, cuts=(), kind=jnp.bfloat16):
    factor_of = level_of(key, extent, cuts, -0.22, 0.18) if cuts else 1.0
    array = jax.random.normal(key, extent, jnp.float32) * spread * factor_of
    return jnp.minimum(jnp.maximum(array, -limit), limit).astype(kind)


def setup_inputs(seed: int = 0) -> dict:
    key_of = jax.random.split(jax.random.key(seed), 7)
    return {
        "positions": centred(key_of[0], (3, SEGS), 1.0, 6.0, ((1, 32),), jnp.float32),
        "line_vectors": centred(key_of[1], (3, SEGS), 1.0, 6.0, ((1, 32),), jnp.float32),
        "burgers": centred(key_of[2], (3, SEGS), 1.0, 6.0, ((1, 32),), jnp.float32),
        "mobility": jnp.clip(jnp.exp(math.log(2.0) - 1.3862944 * jax.random.uniform(key_of[3], (SEGS,), jnp.float32) ** level_of(key_of[3], (SEGS,), ((0, 32),), -0.2, 0.2)), 0.5, 2.0),
        "close_list": draw_close_list(jax.random.fold_in(key_of[6], 71), 0),
        "ghost_map": draw_ghost_map(jax.random.fold_in(key_of[6], 71), 0),
    }


long_core = 1.0
short_core = 0.25
time_step = 0.05

def pair_weights(target, source, core):
    delta_x = target[0][..., :, None] - source[0][..., None, :]
    delta_y = target[1][..., :, None] - source[1][..., None, :]
    delta_z = target[2][..., :, None] - source[2][..., None, :]
    radius = delta_x * delta_x + delta_y * delta_y + delta_z * delta_z + core * core
    inverse = lax.rsqrt(radius)
    line_dot = target[3][..., :, None] * source[3][..., None, :] + target[4][..., :, None] * source[4][..., None, :] + target[5][..., :, None] * source[5][..., None, :]
    burgers_dot = target[6][..., :, None] * source[6][..., None, :] + target[7][..., :, None] * source[7][..., None, :] + target[8][..., :, None] * source[8][..., None, :]
    weight = burgers_dot * line_dot * inverse * inverse * inverse
    return (weight, (delta_x, delta_y, delta_z))

def cell_force(target, source):
    weight, deltas = pair_weights(target, source, long_core)
    return jnp.stack([lax.optimization_barrier(jnp.sum(weight * delta, axis=-1)) for delta in deltas])

def slot_force(own_rows, partners):
    delta_x = own_rows[0][None] - partners[0]
    delta_y = own_rows[1][None] - partners[1]
    delta_z = own_rows[2][None] - partners[2]
    radius = delta_x * delta_x + delta_y * delta_y + delta_z * delta_z + short_core * short_core
    inverse = lax.rsqrt(radius)
    line_dot = own_rows[3][None] * partners[3] + own_rows[4][None] * partners[4] + own_rows[5][None] * partners[5]
    burgers_dot = own_rows[6][None] * partners[6] + own_rows[7][None] * partners[7] + own_rows[8][None] * partners[8]
    weight = burgers_dot * line_dot * inverse * inverse * inverse
    return jnp.stack([lax.optimization_barrier(jnp.sum(weight * delta_x, 0)), lax.optimization_barrier(jnp.sum(weight * delta_y, 0)), lax.optimization_barrier(jnp.sum(weight * delta_z, 0))])

def long_range(seg_state):
    cycle_reach = N_BLK // 4
    device_count = N_BLK * N_DOM
    cell_rows = seg_state.reshape(9, device_count, CELLS, CELL_SEGS)

    def per_device(device):
        block_id = device // N_DOM
        domain = device % N_DOM
        target = jnp.take(cell_rows, device, axis=1)
        summed = cell_force(target, target)
        for offset in range(1, cycle_reach + 1):
            for direction in (1, -1):
                source_dev = (block_id + direction * offset + N_BLK) % N_BLK * N_DOM + domain
                summed = summed + cell_force(target, jnp.take(cell_rows, source_dev, axis=1))
        return summed.reshape(3, -1)
    forces = lax.map(per_device, jnp.arange(device_count, dtype=jnp.int32))
    return jnp.moveaxis(forces, 0, 1).reshape(3, -1) / math.sqrt((2 * cycle_reach + 1) * CELL_SEGS)

def window_places(close_rows):
    seg_index = jnp.arange(SEG_DEV, dtype=jnp.int32)
    cell_index = seg_index // CELL_SEGS
    own_place = cell_index[None, :] * CELL_SEGS + close_rows
    ghost_place = SEG_DEV + cell_index[None, :] % WINDOWS * CELL_SEGS + (close_rows - CELL_SEGS)
    empty_place = SEG_DEV + 2 * GHOSTS
    places = jnp.where(close_rows < CELL_SEGS, own_place, jnp.where(close_rows < 2 * CELL_SEGS, ghost_place, empty_place))
    return places.astype(jnp.int32)

def short_range(current, statics, close_list, map_rows):
    device_count = N_BLK * N_DOM
    full_rows = jnp.concatenate([current, statics], 0).reshape(9, device_count, -1)
    close_rows = close_list.reshape(SLOTS, device_count, -1)

    def per_device(device):
        block_id = device // N_DOM
        domain = device % N_DOM
        lower_dev = block_id * N_DOM + (domain + N_DOM - 1) % N_DOM
        upper_dev = block_id * N_DOM + (domain + 1) % N_DOM
        own_rows = jnp.take(full_rows, device, axis=1)
        from_lower = jnp.take(jnp.take(full_rows, lower_dev, axis=1), jnp.take(map_rows, lower_dev, axis=0)[GHOSTS:], axis=1)
        from_upper = jnp.take(jnp.take(full_rows, upper_dev, axis=1), jnp.take(map_rows, upper_dev, axis=0)[:GHOSTS], axis=1)
        extended_rows = jnp.concatenate([own_rows, from_lower, from_upper], 1)
        places = window_places(jnp.take(close_rows, device, axis=1))
        partners = jnp.take(extended_rows, places, axis=1, mode='fill', fill_value=0.0)
        return slot_force(own_rows, partners)
    forces = lax.map(per_device, jnp.arange(device_count, dtype=jnp.int32))
    return jnp.moveaxis(forces, 0, 1).reshape(3, -1) / math.sqrt(SLOTS)

def reference(positions, line_vectors, burgers, mobility, close_list, ghost_map):
    statics = jnp.concatenate([line_vectors, burgers], 0)
    long_force = long_range(jnp.concatenate([positions, statics], 0))
    velocity = jnp.zeros_like(positions)
    for subcycle in range(SUBS):
        map_rows = ghost_map[subcycle].reshape(N_BLK * N_DOM, 2 * GHOSTS)
        first_vel = mobility * (long_force + short_range(positions, statics, close_list, map_rows))
        guess_pos = positions + time_step * first_vel
        second = mobility * (long_force + short_range(guess_pos, statics, close_list, map_rows))
        velocity = 0.5 * (first_vel + second)
        positions = positions + time_step * velocity
    return (positions, velocity)
```

```python
import math

import jax
import jax.numpy as jnp
from jax import lax
from jax.experimental import pallas as pl
from jax.experimental.pallas import tpu as pltpu
from jax.sharding import PartitionSpec as P

LANES = 128
ROWS = 8
long_core = 1.0
short_core = 0.25
time_step = 0.05


def lane_gather(row_block, places):
    return jnp.take_along_axis(row_block, places, axis=1, mode="promise_in_bounds")


def level_halves(domains, evals):
    levels = [{(0, 0), (0, 1)}]
    for _ in range(evals - 1):
        last = levels[-1]
        grown = set(last)
        for domain in {d for d, _ in last}:
            grown.add(((domain - 1) % domains, 1))
            grown.add(((domain + 1) % domains, 0))
        levels.append(grown)
    return [sorted(level) for level in levels[::-1]]


def step_kernel(domains, subs, ghosts, slots, tables, core_of, *refs):
    half = domains // 2
    pack_refs = refs[: 2 * half]
    close_refs = refs[2 * half : 4 * half]
    dom_table, half_table = refs[4 * half : 4 * half + 2]
    out_pos, out_vel = refs[4 * half + 2 : 4 * half + 4]
    pack, close, own_w, weight, pos, guess, first, long_, ghost, sem = refs[4 * half + 4 :]
    seg = pack.shape[2]
    cells = seg // LANES
    groups = slots // ROWS
    core = core_of()
    half_cells = cells // 2
    windows = 2 * ghosts // LANES
    scale = 1.0 / math.sqrt(slots)

    copies = []
    for j in range(half):
        for other in range(2):
            parity = core if other == 0 else 1 - core
            place = lax.rem(parity + 2 * j, domains)
            for which, (src, dst) in enumerate(((pack_refs, pack), (close_refs, close))):
                copy = pltpu.make_async_copy(src[other * half + j], dst.at[place], sem.at[which, other * half + j])
                copy.start()
                copies.append(copy)
    for copy in copies:
        copy.wait()

    row = lax.broadcasted_iota(jnp.int32, (ROWS, LANES), 0)
    even_row = lax.rem(row, 2) == 0
    x_rows = row < 2
    y_rows = row < 4

    def spread(source, d, at):
        return jnp.concatenate([jnp.broadcast_to(source[d, at + c : at + c + 1, :], (2, seg)) for c in (0, 1, 2, 2)], 0)

    def expand(d, carry):
        pos[d] = spread(pack, d, 0)
        long_[d] = spread(pack, d, 10)
        return carry

    lax.fori_loop(0, domains, expand, 0)

    def bcast(ref, d, at, lane):
        return jnp.broadcast_to(ref[d, at : at + 1, pl.ds(lane, LANES)], (ROWS, LANES))

    def ghost_places(d, sub, upper):
        at = 13 + sub // 2
        lane = (sub % 2) * 2 * ghosts + (0 if upper else ghosts)
        first_w = bcast(pack, d, at, lane)
        second_w = bcast(pack, d, at, lane + LANES)
        return jnp.where(even_row, first_w, second_w).astype(jnp.int32)

    def pick(source_cells, places, first_cell):
        lane = places & (LANES - 1)
        cell = places >> 7
        out = lane_gather(source_cells[0], lane)
        for k in range(1, len(source_cells)):
            out = jnp.where(cell == first_cell + k, lane_gather(source_cells[k], lane), out)
        return out

    def neighbours(d):
        return lax.rem(d + domains - 1, domains), lax.rem(d + 1, domains)

    def pick_ghosts(ref, d, sub):
        low, up = neighbours(d)
        lower = pick(
            [ref[low, :, pl.ds((half_cells + k) * LANES, LANES)] for k in range(half_cells)],
            ghost_places(low, sub, False), half_cells)
        upper = pick(
            [ref[up, :, pl.ds(k * LANES, LANES)] for k in range(half_cells)],
            ghost_places(up, sub, True), 0)
        return lower, upper

    def store_ghosts(ref, d, sub, slot):
        lower, upper = pick_ghosts(ref, d, sub)
        ghost[slot, d, 0] = lower
        ghost[slot, d, 1] = upper

    def dots(mine, theirs):
        return mine[0] * theirs[0] + mine[1] * theirs[1] + mine[2] * theirs[2]

    def own_weights(d, carry):
        for q in range(cells):
            lane = q * LANES
            mine = [bcast(pack, d, 3 + c, lane) for c in range(6)]
            for g in range(groups):
                places = close[d, g * ROWS : (g + 1) * ROWS, pl.ds(lane, LANES)] & (LANES - 1)
                theirs = [lane_gather(m, places) for m in mine]
                own_w[d, g * ROWS : (g + 1) * ROWS, pl.ds(lane, LANES)] = (
                    dots(mine[:3], theirs[:3]) * dots(mine[3:], theirs[3:]) * scale)
        return carry

    lax.fori_loop(0, domains, own_weights, 0)

    def ghost_rows(slot, d, w):
        side, pair = divmod(w, 2)
        return [jnp.broadcast_to(ghost[slot, d, side, 2 * c + pair : 2 * c + pair + 1, :], (ROWS, LANES)) for c in range(3)]

    def where_of(i):
        return lax.rem(dom_table[i] + core, domains), half_table[i]

    def sub_weights(sub, start, stop):
        def one(i, carry):
            d, side = where_of(i)
            low, up = neighbours(d)
            low_places, up_places = ghost_places(low, sub, False), ghost_places(up, sub, True)
            for slot, at in ((1, 3), (2, 6)):
                def cells_of(dom, cell):
                    return [jnp.concatenate([jnp.broadcast_to(pack[dom, at + c : at + c + 1, pl.ds((cell + k) * LANES, LANES)], (2, LANES)) for c in (0, 1, 2, 2)], 0) for k in range(half_cells)]
                ghost[slot, d, 0] = pick(cells_of(low, half_cells), low_places, half_cells)
                ghost[slot, d, 1] = pick(cells_of(up, 0), up_places, 0)
            for k in range(half_cells):
                lane = pl.multiple_of(side * (half_cells * LANES) + k * LANES, LANES)
                mine = [bcast(pack, d, 3 + c, lane) for c in range(6)]
                far = ghost_rows(1, d, k % windows) + ghost_rows(2, d, k % windows)
                for g in range(groups):
                    at = slice(g * ROWS, (g + 1) * ROWS)
                    entry = close[d, at, pl.ds(lane, LANES)]
                    places = entry & (LANES - 1)
                    theirs = [lane_gather(m, places) for m in far]
                    far_w = dots(mine[:3], theirs[:3]) * dots(mine[3:], theirs[3:]) * scale
                    near_w = own_w[d, at, pl.ds(lane, LANES)]
                    weight[d, at, pl.ds(lane, LANES)] = jnp.where(
                        entry < LANES, near_w, jnp.where(entry < 2 * LANES, far_w, 0.0))
            return carry
        lax.fori_loop(start, stop, one, 0)

    def total(block):
        for shift in (4, 2, 1):
            block = block + pltpu.roll(block, shift, 0)
        return block

    def force(ref, d, lane, window):
        mine = [bcast(ref, d, 2 * c, lane) for c in range(3)]
        far = ghost_rows(0, d, window)
        sums = [None] * 3
        for g in range(groups):
            at = slice(g * ROWS, (g + 1) * ROWS)
            entry = close[d, at, pl.ds(lane, LANES)]
            places = entry & (LANES - 1)
            near = entry < LANES
            delta = [m - jnp.where(near, lane_gather(m, places), lane_gather(f, places)) for m, f in zip(mine, far)]
            radius = delta[0] * delta[0] + delta[1] * delta[1] + delta[2] * delta[2] + short_core * short_core
            inverse = lax.rsqrt(radius)
            w = weight[d, at, pl.ds(lane, LANES)] * (inverse * inverse * inverse)
            for c in range(3):
                term = w * delta[c]
                sums[c] = term if sums[c] is None else sums[c] + term
        sums = [total(s) for s in sums]
        return jnp.where(x_rows, sums[0], jnp.where(y_rows, sums[1], sums[2]))

    at = 0
    for sub in range(subs):
        for stage in range(2):
            start, stop, doms = tables[2 * sub + stage]
            source = guess if stage else pos
            if stage == 0:
                sub_weights(sub, start, stop)

            def ghosts_one(i, carry):
                store_ghosts(source, lax.rem(dom_table[i] + core, domains), sub, 0)
                return carry

            lax.fori_loop(doms[0], doms[1], ghosts_one, 0)

            def one(i, carry):
                d, side = where_of(i)
                for k in range(half_cells):
                    lane = pl.multiple_of(side * (half_cells * LANES) + k * LANES, LANES)
                    here = pl.ds(lane, LANES)
                    mob = bcast(pack, d, 9, lane)
                    vel = mob * (long_[d, :, here] + force(source, d, lane, k % windows))
                    if stage == 0:
                        first[d, :, here] = vel
                        guess[d, :, here] = pos[d, :, here] + time_step * vel
                    else:
                        vel = 0.5 * (first[d, :, here] + vel)
                        first[d, :, here] = vel
                        pos[d, :, here] = pos[d, :, here] + time_step * vel
                return carry

            lax.fori_loop(start, stop, one, 0)

    for c in range(3):
        out_pos[c : c + 1, :] = pos[core, 2 * c : 2 * c + 1, :]
        out_vel[c : c + 1, :] = first[core, 2 * c : 2 * c + 1, :]


def step(packs, closes, subs, ghosts, core_of):
    domains = len(packs)
    slots, seg = closes[0].shape
    rows = packs[0].shape[0]
    dom_list, half_list, tables = [], [], []
    for level in level_halves(domains, 2 * subs):
        start = len(dom_list)
        dom_list += [d for d, _ in level]
        half_list += [h for _, h in level]
        stop = len(dom_list)
        doms = sorted({d for d, _ in level})
        dom_list += doms
        half_list += [0] * len(doms)
        tables.append((start, stop, (stop, len(dom_list))))
    table = pl.BlockSpec(memory_space=pltpu.SMEM)
    far = pl.BlockSpec(memory_space=pl.ANY)
    wide = pltpu.VMEM((domains, slots, seg), jnp.float32)
    state = pltpu.VMEM((domains, ROWS, seg), jnp.float32)

    def kernel(*refs):
        step_kernel(domains, subs, ghosts, slots, tables, core_of, *refs)

    return pl.pallas_call(
        kernel,
        out_shape=[jax.ShapeDtypeStruct((3, seg), jnp.float32)] * 2,
        in_specs=[far] * (2 * domains) + [table] * 2,
        out_specs=[pl.BlockSpec(memory_space=pltpu.VMEM)] * 2,
        scratch_shapes=[
            pltpu.VMEM((domains, rows, seg), jnp.float32),
            pltpu.VMEM((domains, slots, seg), jnp.int32),
            wide, wide, state, state, state, state,
            pltpu.VMEM((3, domains, 2, ROWS, LANES), jnp.float32),
            pltpu.SemaphoreType.DMA((2, domains)),
        ],
        compiler_params=pltpu.CompilerParams(vmem_limit_bytes=48 * 2**20),
        name="step",
    )(*packs, *closes, jnp.array(dom_list, jnp.int32), jnp.array(half_list, jnp.int32))


def long_kernel(sources, seg, *refs):
    own = refs[:3]
    mob, gmap = refs[3:5]
    others = refs[5 : 5 + sources]
    pack, tiles = refs[5 + sources :]
    cells = seg // LANES
    scale = 1.0 / math.sqrt((sources + 1) * LANES)
    for s in range(sources + 1):
        for c in range(9):
            for q in range(cells):
                src = own[c // 3][c % 3 : c % 3 + 1, q * LANES : (q + 1) * LANES] if s == 0 else others[s - 1][c : c + 1, q * LANES : (q + 1) * LANES]
                tiles[s * 9 + c, q : q + 1, :] = src
    mine = [tiles[c] for c in range(9)]

    def one(i, carry):
        forces, moved = carry
        forces = list(forces)
        for s in range(sources + 1):
            other = moved[s * 9 : s * 9 + 9]
            delta = [mine[c] - other[c] for c in range(3)]
            radius = delta[0] * delta[0] + delta[1] * delta[1] + delta[2] * delta[2] + long_core * long_core
            inverse = lax.rsqrt(radius)
            line = mine[3] * other[3] + mine[4] * other[4] + mine[5] * other[5]
            burg = mine[6] * other[6] + mine[7] * other[7] + mine[8] * other[8]
            w = burg * line * (inverse * inverse * inverse)
            for c in range(3):
                forces[c] = forces[c] + w * delta[c]
        return tuple(forces), tuple(pltpu.roll(m, 1, 1) for m in moved)

    zero = jnp.zeros_like(mine[0])
    moved = tuple(tiles[k] for k in range(9 * (sources + 1)))
    forces, _ = lax.fori_loop(0, LANES, one, ((zero,) * 3, moved))
    for c in range(9):
        pack[c : c + 1, :] = own[c // 3][c % 3 : c % 3 + 1, :]
    pack[9:10, :] = mob[...]
    for c in range(3):
        f = forces[c] * scale
        for q in range(cells):
            pack[10 + c : 11 + c, q * LANES : (q + 1) * LANES] = f[q : q + 1, :]
    subs, wide = gmap.shape
    per = seg // wide
    for t in range(subs):
        pack[13 + t // per : 14 + t // per, (t % per) * wide : (t % per + 1) * wide] = gmap[t : t + 1, :].astype(jnp.float32)


def long_range(positions, line_vectors, burgers, mobility, ghost_map, others):
    seg = positions.shape[1]
    return pl.pallas_call(
        lambda *refs: long_kernel(len(others), seg, *refs),
        out_shape=jax.ShapeDtypeStruct((16, seg), jnp.float32),
        in_specs=[pl.BlockSpec(memory_space=pltpu.VMEM)] * (5 + len(others)),
        out_specs=pl.BlockSpec(memory_space=pltpu.VMEM),
        scratch_shapes=[pltpu.VMEM((9 * (len(others) + 1), seg // LANES, LANES), jnp.float32)],
        name="long_range",
    )(positions, line_vectors, burgers, mobility.reshape(1, -1), ghost_map, *others)


def shifted(value, axis, steps):
    count = lax.axis_size(axis)
    return lax.ppermute(value, axis, [(i, (i + steps) % count) for i in range(count)])


def swapped(value, axis):
    count = lax.axis_size(axis)
    return lax.ppermute(value, axis, [(i, i ^ 1) for i in range(count)])


def local(positions, line_vectors, burgers, mobility, close_list, ghost_map):
    subs = ghost_map.shape[0]
    ghosts = ghost_map.shape[1] // 2
    domains = lax.axis_size("dom")
    reach = lax.axis_size("blk") // 4
    state = jnp.concatenate([positions, line_vectors, burgers], 0)
    others = [shifted(state, "blk", s * k) for k in range(1, reach + 1) for s in (1, -1)]
    closes = [close_list] + [shifted(close_list, "dom", -2 * j) for j in range(1, domains // 2)]
    closes += [swapped(c, "dom") for c in closes]
    pack = long_range(positions, line_vectors, burgers, mobility, ghost_map, others)
    packs = [pack] + [shifted(pack, "dom", -2 * j) for j in range(1, domains // 2)]
    packs += [swapped(p, "dom") for p in packs]
    core_of = lambda: lax.rem(lax.axis_index("dom"), 2)
    return tuple(step(packs, closes, subs, ghosts, core_of))


def solution(mesh):
    spread = P(None, ("blk", "dom"))
    return jax.shard_map(
        local,
        mesh=mesh,
        in_specs=(spread, spread, spread, P(("blk", "dom")), spread, spread),
        out_specs=(spread, spread),
        check_vma=False,
    )
```

```python
import math

import jax
import jax.numpy as jnp
from jax import lax
from jax.experimental import pallas as pl
from jax.experimental.pallas import tpu as pltpu
from jax.sharding import PartitionSpec as P

LANES = 128
ROWS = 8
long_core = 1.0
short_core = 0.25
time_step = 0.05


def lane_gather(row_block, places):
    return jnp.take_along_axis(row_block, places, axis=1, mode="promise_in_bounds")


def level_halves(domains, evals):
    levels = [{(0, 0), (0, 1)}]
    for _ in range(evals - 1):
        last = levels[-1]
        grown = set(last)
        for domain in {d for d, _ in last}:
            grown.add(((domain - 1) % domains, 1))
            grown.add(((domain + 1) % domains, 0))
        levels.append(grown)
    return [sorted(level) for level in levels[::-1]]


WEIGHT_VMEM = 24
STEP_VMEM = 24

def fetch(refs, held, me, sem):
    half = len(refs) // 2
    copies = []
    for j in range(half):
        for other in range(2):
            at = other * half + j
            copies.append(pltpu.make_async_copy(refs[at], held.at[me ^ (2 * j + other)], sem.at[at]))
    for copy in copies:
        copy.start()
    for copy in copies:
        copy.wait()


def weights_kernel(domains, slots, subs, plan, own_index, *refs):
    block_refs = refs[:domains]
    dom_table, half_table = refs[domains : domains + 2]
    weight, close, gplaces, pack, still_rows, still, sem = refs[domains + 2 :]
    seg = pack.shape[2]
    cells = seg // LANES
    groups = slots // ROWS
    half_cells = cells // 2
    half_lanes = half_cells * LANES
    ghosts = seg // (2 * (subs // 2))
    me = own_index()
    scale = 1.0 / math.sqrt(slots)
    LINE, BURG, GHOST = slots, slots + 3, slots + 6
    fetch(block_refs, pack, me, sem)

    row = lax.broadcasted_iota(jnp.int32, (ROWS, LANES), 0)
    x_rows = row < 2
    y_rows = row < 4

    even_row = lax.rem(row, 2) == 0

    def bcast(ref, index, at, lane):
        return jnp.broadcast_to(ref[*index, at : at + 1, pl.ds(lane, LANES)], (ROWS, LANES))

    def spread(ref, d, at, lane):
        x, y, z = (bcast(ref, (d,), at + c, lane) for c in range(3))
        return jnp.where(x_rows, x, jnp.where(y_rows, y, z))

    def expand(d, carry):
        for q in range(cells):
            here = pl.ds(q * LANES, LANES)
            for at, slot in ((LINE, 0), (BURG, 1)):
                still_rows[slot, d, :, here] = spread(pack, d, at, q * LANES)
        for sub in range(subs):
            for side in range(2):
                lane = (sub % 2) * 2 * ghosts + side * ghosts
                at = GHOST + sub // 2
                place = jnp.where(even_row, bcast(pack, (d,), at, lane), bcast(pack, (d,), at, lane + LANES))
                gplaces[d, :, pl.ds((2 * sub + side) * LANES, LANES)] = place.astype(jnp.int32)
        return carry

    lax.fori_loop(0, domains, expand, 0)

    def domain_at(i):
        return lax.rem(dom_table[i] + me, domains)

    def owner_picks(i, count, sub, sources):
        made = []
        for u in range(count):
            d = domain_at(i + u)
            for side in range(2):
                place = gplaces[d, :, pl.ds(pl.multiple_of((2 * sub + side) * LANES, LANES), LANES)]
                lane = place & (LANES - 1)
                cell = place >> 7
                to = lax.rem(d + (1 if side else domains - 1), domains)
                for source, ref, slot in sources:
                    out = None
                    for k in range(half_cells):
                        got = lane_gather(source[d, :, pl.ds(side * half_lanes + k * LANES, LANES)], lane)
                        out = got if out is None else jnp.where(cell == side * half_cells + k, got, out)
                    made.append((ref, slot, to, 1 - side, out))
        for ref, slot, to, at, out in made:
            ref[*slot, to, at] = out

    def over(span, body):
        start, steps, count = span
        if steps == 1:
            body(start, count)
            return
        def one(i, carry):
            body(start + i * count, count)
            return carry
        lax.fori_loop(0, steps, one, 0)

    def items(i, count):
        for u in range(count):
            d = domain_at(i + u)
            for k in range(half_cells):
                yield d, pl.multiple_of(half_table[i + u] * half_lanes + k * LANES, LANES), k

    def dots(mine, theirs):
        return mine[0] * theirs[0] + mine[1] * theirs[1] + mine[2] * theirs[2]

    def pair_weight(mine, source, places):
        theirs = [lane_gather(m, places) for m in source]
        return dots(mine[:3], theirs[:3]) * dots(mine[3:], theirs[3:]) * scale

    def ghost_rows(ref, slot, d, k):
        side, pair = divmod(k, 2)
        return [bcast(ref, (*slot, d, side), 2 * c + pair, 0) for c in range(3)]

    def blocks(d, lane):
        for g in range(groups):
            yield (d, slice(g * ROWS, (g + 1) * ROWS), pl.ds(lane, LANES))

    def weights(i, count, upto):
        made = []
        for d, lane, k in items(i, count):
            mine = [bcast(pack, (d,), LINE + c, lane) for c in range(6)]
            far = [ghost_rows(still, (sub, 0), d, k) + ghost_rows(still, (sub, 1), d, k) for sub in range(upto)]
            for at in blocks(d, lane):
                entry = pack[at].astype(jnp.int32)
                places = entry & (LANES - 1)
                near, held = entry < LANES, entry < 2 * LANES
                near_w = pair_weight(mine, mine, places)
                made.append((close.at[at], entry))
                for sub in range(upto):
                    made.append((weight.at[(sub, *at)], jnp.where(near, near_w, jnp.where(held, pair_weight(mine, far[sub], places), 0.0))))
        for ref, value in made:
            ref[...] = value

    for sub in range(subs):
        over(plan["still"][sub], lambda i, count: owner_picks(i, count, sub, ((still_rows.at[0], still, (sub, 0)), (still_rows.at[1], still, (sub, 1)))))
    for upto, span in plan["weights"]:
        over(span, lambda i, count: weights(i, count, upto))


def step_kernel(domains, slots, subs, plan, own_index, *refs):
    now_refs = refs[:domains]
    weight, close, gplaces, dom_table, half_table = refs[domains : domains + 5]
    out_pos, out_vel = refs[domains + 5 : domains + 7]
    now, state, vels, long_, ghost, sem = refs[domains + 7 :]
    seg = now.shape[2]
    evals = vels.shape[0]
    cells = seg // LANES
    groups = slots // ROWS
    half_cells = cells // 2
    half_lanes = half_cells * LANES
    me = own_index()
    POS, MOB, FAR = 0, 3, 4
    fetch(now_refs, now, me, sem)

    row = lax.broadcasted_iota(jnp.int32, (ROWS, LANES), 0)
    x_rows = row < 2
    y_rows = row < 4

    def bcast(ref, index, at, lane):
        return jnp.broadcast_to(ref[*index, at : at + 1, pl.ds(lane, LANES)], (ROWS, LANES))

    def spread(d, at, lane):
        x, y, z = (bcast(now, (d,), at + c, lane) for c in range(3))
        return jnp.where(x_rows, x, jnp.where(y_rows, y, z))

    def expand(d, carry):
        for q in range(cells):
            here = pl.ds(q * LANES, LANES)
            state[0, d, :, here] = spread(d, POS, q * LANES)
            long_[d, :, here] = spread(d, FAR, q * LANES)
        return carry

    lax.fori_loop(0, domains, expand, 0)

    def domain_at(i):
        return lax.rem(dom_table[i] + me, domains)

    def owner_picks(i, count, sub, sources):
        made = []
        for u in range(count):
            d = domain_at(i + u)
            for side in range(2):
                place = gplaces[d, :, pl.ds(pl.multiple_of((2 * sub + side) * LANES, LANES), LANES)]
                lane = place & (LANES - 1)
                cell = place >> 7
                to = lax.rem(d + (1 if side else domains - 1), domains)
                for source, ref, slot in sources:
                    out = None
                    for k in range(half_cells):
                        got = lane_gather(source[d, :, pl.ds(side * half_lanes + k * LANES, LANES)], lane)
                        out = got if out is None else jnp.where(cell == side * half_cells + k, got, out)
                    made.append((ref, slot, to, 1 - side, out))
        for ref, slot, to, at, out in made:
            ref[*slot, to, at] = out

    def over(span, body):
        start, steps, count = span
        if steps == 1:
            body(start, count)
            return
        def one(i, carry):
            body(start + i * count, count)
            return carry
        lax.fori_loop(0, steps, one, 0)

    def items(i, count):
        for u in range(count):
            d = domain_at(i + u)
            for k in range(half_cells):
                yield d, pl.multiple_of(half_table[i + u] * half_lanes + k * LANES, LANES), k

    def ghost_rows(ref, slot, d, k):
        side, pair = divmod(k, 2)
        return [bcast(ref, (*slot, d, side), 2 * c + pair, 0) for c in range(3)]

    def blocks(d, lane):
        for g in range(groups):
            yield (d, slice(g * ROWS, (g + 1) * ROWS), pl.ds(lane, LANES))

    def total(block):
        for shift in (4, 2, 1):
            block = block + pltpu.roll(block, shift, 0)
        return block

    def force(level, sub, d, lane, k):
        mine = [bcast(state, (level, d), 2 * c, lane) for c in range(3)]
        far = ghost_rows(ghost, (), d, k)
        sums = [None] * 3
        for at in blocks(d, lane):
            entry = close[at]
            places = entry & (LANES - 1)
            near = entry < LANES
            delta = [m - jnp.where(near, lane_gather(m, places), lane_gather(f, places)) for m, f in zip(mine, far)]
            radius = delta[0] * delta[0] + delta[1] * delta[1] + delta[2] * delta[2] + short_core * short_core
            inverse = lax.rsqrt(radius)
            w = weight[(sub, *at)] * (inverse * inverse * inverse)
            for c in range(3):
                term = w * delta[c]
                sums[c] = term if sums[c] is None else sums[c] + term
        sums = [total(s) for s in sums]
        return jnp.where(x_rows, sums[0], jnp.where(y_rows, sums[1], sums[2]))

    def evaluate(level, owners, halves):
        sub = level // 2
        stage = lax.rem(level, 2)
        base = level - stage
        over(owners, lambda i, count: owner_picks(i, count, sub, ((state.at[level], ghost, ()),)))

        def one(i, count):
            made = []
            for d, lane, k in items(i, count):
                here = pl.ds(lane, LANES)
                vel = bcast(now, (d,), MOB, lane) * (long_[d, :, here] + force(level, sub, d, lane, k))
                vel = jnp.where(stage == 1, 0.5 * (vels[base, d, :, here] + vel), vel)
                made.append((d, here, vel, state[base, d, :, here] + time_step * vel))
            for d, here, vel, moved in made:
                vels[level, d, :, here] = vel
                state[level + 1, d, :, here] = moved

        over(halves, one)

    for first, last, owners, halves in plan["levels"]:
        if last - first == 1:
            evaluate(jnp.int32(first), owners, halves)
        else:
            lax.fori_loop(first, last, lambda level, carry: (evaluate(level, owners, halves), carry)[1], 0)

    for c in range(3):
        out_pos[c : c + 1, :] = state[evals, me, 2 * c : 2 * c + 1, :]
        out_vel[c : c + 1, :] = vels[evals - 1, me, 2 * c : 2 * c + 1, :]


class Plan:
    def __init__(self):
        self.domains, self.halves = [], []

    def span(self, entries, limit):
        count = min(range(1, limit + 1), key=lambda c: (-(-len(entries) // c) * (c + 0.5), c))
        start, steps = len(self.domains), -(-len(entries) // count)
        entries = entries + [entries[-1]] * (steps * count - len(entries))
        self.domains.extend(d for d, _ in entries)
        self.halves.extend(h for _, h in entries)
        return start, steps, count

    def tables(self):
        return jnp.array(self.domains, jnp.int32), jnp.array(self.halves, jnp.int32)


def owners_of(level, domains):
    return sorted({((d + s) % domains, 0) for d, _ in level for s in (1, -1)})


TABLE = pl.BlockSpec(memory_space=pltpu.SMEM)
ANYWHERE = pl.BlockSpec(memory_space=pl.ANY)
VMEM = pl.BlockSpec(memory_space=pltpu.VMEM)


def pair_weights(blocks, slots, subs, own_index, most=2, most_owners=4):
    domains = len(blocks)
    rows, seg = blocks[0].shape
    levels = level_halves(domains, 2 * subs)
    table = Plan()
    plan = {"still": [table.span(owners_of(levels[2 * t], domains), most_owners) for t in range(subs)], "weights": []}
    for upto in range(1, subs + 1):
        after = levels[2 * upto] if upto < subs else []
        only = [h for h in levels[2 * upto - 2] if h not in after]
        if only:
            plan["weights"].append((upto, table.span(only, most)))

    def kernel(*refs):
        weights_kernel(domains, slots, subs, plan, own_index, *refs)

    return pl.pallas_call(
        kernel,
        out_shape=[
            jax.ShapeDtypeStruct((subs, domains, slots, seg), jnp.float32),
            jax.ShapeDtypeStruct((domains, slots, seg), jnp.int32),
            jax.ShapeDtypeStruct((domains, ROWS, seg), jnp.int32),
        ],
        in_specs=[ANYWHERE] * domains + [TABLE] * 2,
        out_specs=[VMEM] * 3,
        scratch_shapes=[
            pltpu.VMEM((domains, rows, seg), jnp.float32),
            pltpu.VMEM((2, domains, ROWS, seg), jnp.float32),
            pltpu.VMEM((subs, 2, domains, 2, ROWS, LANES), jnp.float32),
            pltpu.SemaphoreType.DMA((domains,)),
        ],
        compiler_params=pltpu.CompilerParams(vmem_limit_bytes=WEIGHT_VMEM * 2**20),
        cost_estimate=pl.CostEstimate(flops=10**7, bytes_accessed=4 * 10**7, transcendentals=0),
        name="weights",
    )(*blocks, *table.tables())


def step(now, weights, subs, own_index, most=8, most_owners=8):
    domains = len(now)
    rows, seg = now[0].shape
    slots = weights[0].shape[2]
    levels = level_halves(domains, 2 * subs)
    table = Plan()
    plan = {"levels": []}
    first = 0
    while first < len(levels):
        last = first + 1
        while last < len(levels) and levels[last] == levels[first]:
            last += 1
        plan["levels"].append((first, last, table.span(owners_of(levels[first], domains), most_owners), table.span(levels[first], most)))
        first = last

    def kernel(*refs):
        step_kernel(domains, slots, subs, plan, own_index, *refs)

    return pl.pallas_call(
        kernel,
        out_shape=[jax.ShapeDtypeStruct((3, seg), jnp.float32)] * 2,
        in_specs=[ANYWHERE] * domains + [VMEM] * 3 + [TABLE] * 2,
        out_specs=[VMEM] * 2,
        scratch_shapes=[
            pltpu.VMEM((domains, rows, seg), jnp.float32),
            pltpu.VMEM((2 * subs + 1, domains, ROWS, seg), jnp.float32),
            pltpu.VMEM((2 * subs, domains, ROWS, seg), jnp.float32),
            pltpu.VMEM((domains, ROWS, seg), jnp.float32),
            pltpu.VMEM((domains, 2, ROWS, LANES), jnp.float32),
            pltpu.SemaphoreType.DMA((domains,)),
        ],
        compiler_params=pltpu.CompilerParams(vmem_limit_bytes=STEP_VMEM * 2**20),
        cost_estimate=pl.CostEstimate(flops=10**7, bytes_accessed=6 * 10**7, transcendentals=10**6),
        name="step",
    )(*now, *weights, *table.tables())


def long_kernel(sources, seg, *refs):
    own, mob = refs[:3], refs[3]
    others = refs[4 : 4 + sources]
    out, tiles = refs[4 + sources :]
    cells = seg // LANES
    unroll = 16
    scale = 1.0 / math.sqrt((sources + 1) * LANES)
    for s in range(sources + 1):
        for c in range(9):
            for q in range(cells):
                src = own[c // 3][c % 3 : c % 3 + 1, q * LANES : (q + 1) * LANES] if s == 0 else others[s - 1][c : c + 1, q * LANES : (q + 1) * LANES]
                tiles[s * 9 + c, q : q + 1, :] = src
    mine = [tiles[c] for c in range(9)]

    def one(i, forces):
        forces = list(forces)
        for s in range(sources + 1):
            for u in range(unroll):
                other = [pltpu.roll(tiles[s * 9 + c], i * unroll + u, 1) for c in range(9)]
                delta = [mine[c] - other[c] for c in range(3)]
                radius = delta[0] * delta[0] + delta[1] * delta[1] + delta[2] * delta[2] + long_core * long_core
                inverse = lax.rsqrt(radius)
                line = mine[3] * other[3] + mine[4] * other[4] + mine[5] * other[5]
                burg = mine[6] * other[6] + mine[7] * other[7] + mine[8] * other[8]
                w = burg * line * (inverse * inverse * inverse)
                for c in range(3):
                    forces[c] = forces[c] + w * delta[c]
        return tuple(forces)

    out[0:3, :] = own[0][...]
    out[3:4, :] = mob[...]
    zero = jnp.zeros_like(mine[0])
    forces = lax.fori_loop(0, LANES // unroll, one, (zero,) * 3)
    for c in range(3):
        for q in range(cells):
            out[4 + c : 5 + c, q * LANES : (q + 1) * LANES] = forces[c][q : q + 1, :] * scale


def long_range(positions, line_vectors, burgers, mobility, others):
    seg = positions.shape[1]
    return pl.pallas_call(
        lambda *refs: long_kernel(len(others), seg, *refs),
        out_shape=jax.ShapeDtypeStruct((ROWS, seg), jnp.float32),
        in_specs=[pl.BlockSpec(memory_space=pltpu.VMEM)] * (4 + len(others)),
        out_specs=pl.BlockSpec(memory_space=pltpu.VMEM),
        scratch_shapes=[pltpu.VMEM((9 * (len(others) + 1), seg // LANES, LANES), jnp.float32)],
        cost_estimate=pl.CostEstimate(flops=10**7, bytes_accessed=2 * 10**7, transcendentals=10**6),
        name="long_range",
    )(positions, line_vectors, burgers, mobility[None], *others)


def shifted(value, axis, steps):
    count = lax.axis_size(axis)
    return lax.ppermute(value, axis, [(i, (i + steps) % count) for i in range(count)])


def matched(value, axis, step):
    count = lax.axis_size(axis)
    return lax.ppermute(value, axis, [(i, i ^ step) for i in range(count)])


def cycle_neighbours(value, axis):
    count = lax.axis_size(axis)
    got = [matched(value, axis, 1), lax.ppermute(value, axis, [(i, (((i - 1) % count) ^ 1) + 1 if ((i - 1) % count) ^ 1 != count - 1 else 0) for i in range(count)])]
    for k in range(2, count // 4 + 1):
        got += [shifted(value, axis, k), shifted(value, axis, -k)]
    return got


def along_chips(value):
    return [value] + [matched(value, "dom", 2 * j) for j in range(1, lax.axis_size("dom") // 2)]


def local(positions, line_vectors, burgers, mobility, close_list, ghost_map):
    slots, seg = close_list.shape
    subs = ghost_map.shape[0]
    own_index = lambda: lax.axis_index("dom")
    state = jnp.concatenate([positions, line_vectors, burgers], 0)
    others = cycle_neighbours(state, "blk")
    block = jnp.concatenate([close_list.astype(jnp.float32), line_vectors, burgers, ghost_map.astype(jnp.float32).reshape(-1, seg)], 0)
    blocks = along_chips(block)
    now = long_range(positions, line_vectors, burgers, mobility, others)
    blocks, now = lax.optimization_barrier((blocks, now))
    nows = along_chips(now)
    blocks = blocks + [matched(b, "dom", 1) for b in blocks]
    weights = pair_weights(blocks, slots, subs, own_index)
    nows, weights = lax.optimization_barrier((nows, weights))
    nows = nows + [matched(n, "dom", 1) for n in nows]
    return tuple(step(nows, weights, subs, own_index))


def solution(mesh):
    spread = P(None, ("blk", "dom"))
    return jax.shard_map(
        local,
        mesh=mesh,
        in_specs=(spread, spread, spread, P(("blk", "dom")), spread, spread),
        out_specs=(spread, spread),
        check_vma=False,
    )
```

```python
import math

import jax
import jax.numpy as jnp
from jax import lax
from jax.experimental import pallas as pl
from jax.experimental.pallas import tpu as pltpu
from jax.sharding import PartitionSpec as P

LANES = 128
ROWS = 8
long_core = 1.0
short_core = 0.25
time_step = 0.05


def lane_gather(row_block, places):
    return jnp.take_along_axis(row_block, places, axis=1, mode="promise_in_bounds")


def level_halves(domains, evals):
    levels = [{(0, 0), (0, 1)}]
    for _ in range(evals - 1):
        last = levels[-1]
        grown = set(last)
        for domain in {d for d, _ in last}:
            grown.add(((domain - 1) % domains, 1))
            grown.add(((domain + 1) % domains, 0))
        levels.append(grown)
    return [sorted(level) for level in levels[::-1]]


SMALL_VMEM = 8
PACK_VMEM = 60
WEIGHT_VMEM = 24
STEP_VMEM = 24

def fetch(refs, held, me, sem, order):
    half = len(refs) // 2
    copies = []
    for j in range(half):
        for other in range(2):
            at = other * half + j
            copies.append(pltpu.make_async_copy(refs[at], held.at[me ^ (2 * order[j] + other)], sem.at[at]))
    for copy in copies:
        copy.start()
    for copy in copies:
        copy.wait()


def weights_kernel(domains, slots, subs, plan, own_index, *refs):
    block_refs = refs[:domains]
    weight, close, gplaces, pack, still_rows, still, sem = refs[domains:]
    seg = pack.shape[2]
    cells = seg // LANES
    groups = slots // ROWS
    half_cells = cells // 2
    half_lanes = half_cells * LANES
    ghosts = seg // (2 * (subs // 2))
    me = own_index()
    scale = 1.0 / math.sqrt(slots)
    LINE, BURG, GHOST = slots, slots + 3, slots + 6
    fetch(block_refs, pack, me, sem, [0, *range(domains // 2 - 1, 0, -1)])

    row = lax.broadcasted_iota(jnp.int32, (ROWS, LANES), 0)
    x_rows = row < 2
    y_rows = row < 4

    even_row = lax.rem(row, 2) == 0

    def bcast(ref, index, at, lane):
        return jnp.broadcast_to(ref[*index, at : at + 1, pl.ds(lane, LANES)], (ROWS, LANES))

    def spread(ref, d, at, lane):
        x, y, z = (bcast(ref, (d,), at + c, lane) for c in range(3))
        return jnp.where(x_rows, x, jnp.where(y_rows, y, z))

    def expand(d, carry):
        for q in range(cells):
            here = pl.ds(q * LANES, LANES)
            for at, slot in ((LINE, 0), (BURG, 1)):
                still_rows[slot, d, :, here] = spread(pack, d, at, q * LANES)
        for sub in range(subs):
            for side in range(2):
                lane = (sub % 2) * 2 * ghosts + side * ghosts
                at = GHOST + sub // 2
                place = jnp.where(even_row, bcast(pack, (d,), at, lane), bcast(pack, (d,), at, lane + LANES))
                gplaces[d, :, pl.ds((2 * sub + side) * LANES, LANES)] = place.astype(jnp.int32)
        return carry

    lax.fori_loop(0, domains, expand, 0)

    def domain_of(offset):
        return lax.rem(offset + me, domains)

    def owner_picks(owners, sub, sources):
        made = []
        for offset, _ in owners:
            d = domain_of(offset)
            for side in range(2):
                place = gplaces[d, :, pl.ds(pl.multiple_of((2 * sub + side) * LANES, LANES), LANES)]
                lane = place & (LANES - 1)
                cell = place >> 7
                to = lax.rem(d + (1 if side else domains - 1), domains)
                for source, ref, slot in sources:
                    out = None
                    for k in range(half_cells):
                        got = lane_gather(source[d, :, pl.ds(side * half_lanes + k * LANES, LANES)], lane)
                        out = got if out is None else jnp.where(cell == side * half_cells + k, got, out)
                    made.append((ref, slot, to, 1 - side, out))
        for ref, slot, to, at, out in made:
            ref[*slot, to, at] = out

    def over(span, body):
        steps, count, entries = span
        if steps == 1:
            body(entries)
            return
        def one(i, carry):
            body([tuple(chosen(i, [entries[n * count + u][at] for n in range(steps)]) for at in (0, 1)) for u in range(count)])
            return carry
        lax.fori_loop(0, steps, one, 0)

    def items(entries):
        for offset, side in entries:
            d = domain_of(offset)
            for k in range(half_cells):
                lane = side * half_lanes + k * LANES
                yield d, lane if isinstance(lane, int) else pl.multiple_of(lane, LANES), k

    def dots(mine, theirs):
        return mine[0] * theirs[0] + mine[1] * theirs[1] + mine[2] * theirs[2]

    def pair_weight(mine, source, places):
        theirs = [lane_gather(m, places) for m in source]
        return dots(mine[:3], theirs[:3]) * dots(mine[3:], theirs[3:]) * scale

    def ghost_rows(ref, slot, d, k):
        side, pair = divmod(k, 2)
        return [bcast(ref, (*slot, d, side), 2 * c + pair, 0) for c in range(3)]

    def blocks(d, lane):
        for g in range(groups):
            yield (d, slice(g * ROWS, (g + 1) * ROWS), pl.ds(lane, LANES))

    def weights(entries, upto):
        made = []
        for d, lane, k in items(entries):
            mine = [bcast(pack, (d,), LINE + c, lane) for c in range(6)]
            far = [ghost_rows(still, (sub, 0), d, k) + ghost_rows(still, (sub, 1), d, k) for sub in range(upto)]
            for at in blocks(d, lane):
                entry = pack[at].astype(jnp.int32)
                places = entry & (LANES - 1)
                near, held = entry < LANES, entry < 2 * LANES
                near_w = pair_weight(mine, mine, places)
                made.append((close.at[at], entry))
                for sub in range(upto):
                    made.append((weight.at[(sub, *at)], jnp.where(near, near_w, jnp.where(held, pair_weight(mine, far[sub], places), 0.0))))
        for ref, value in made:
            ref[...] = value

    for sub in range(subs):
        over(plan["still"][sub], lambda owners: owner_picks(owners, sub, ((still_rows.at[0], still, (sub, 0)), (still_rows.at[1], still, (sub, 1)))))
    for upto, span in plan["weights"]:
        over(span, lambda entries: weights(entries, upto))


def step_kernel(domains, slots, subs, plan, own_index, *refs):
    now_refs = refs[:domains]
    weight, close, gplaces = refs[domains : domains + 3]
    out_pos, out_vel = refs[domains + 3 : domains + 5]
    now, state, vels, long_, ghost, sem = refs[domains + 5 :]
    seg = now.shape[2]
    evals = vels.shape[0]
    cells = seg // LANES
    groups = slots // ROWS
    half_cells = cells // 2
    half_lanes = half_cells * LANES
    me = own_index()
    POS, MOB, FAR = 0, 3, 4
    fetch(now_refs, now, me, sem, range(domains // 2))

    row = lax.broadcasted_iota(jnp.int32, (ROWS, LANES), 0)
    x_rows = row < 2
    y_rows = row < 4

    def bcast(ref, index, at, lane):
        return jnp.broadcast_to(ref[*index, at : at + 1, pl.ds(lane, LANES)], (ROWS, LANES))

    def spread(d, at, lane):
        x, y, z = (bcast(now, (d,), at + c, lane) for c in range(3))
        return jnp.where(x_rows, x, jnp.where(y_rows, y, z))

    def expand(d, carry):
        for q in range(cells):
            here = pl.ds(q * LANES, LANES)
            state[0, d, :, here] = spread(d, POS, q * LANES)
            long_[d, :, here] = spread(d, FAR, q * LANES)
        return carry

    lax.fori_loop(0, domains, expand, 0)

    def domain_of(offset):
        return lax.rem(offset + me, domains)

    def owner_picks(owners, sub, sources):
        made = []
        for offset, _ in owners:
            d = domain_of(offset)
            for side in range(2):
                place = gplaces[d, :, pl.ds(pl.multiple_of((2 * sub + side) * LANES, LANES), LANES)]
                lane = place & (LANES - 1)
                cell = place >> 7
                to = lax.rem(d + (1 if side else domains - 1), domains)
                for source, ref, slot in sources:
                    out = None
                    for k in range(half_cells):
                        got = lane_gather(source[d, :, pl.ds(side * half_lanes + k * LANES, LANES)], lane)
                        out = got if out is None else jnp.where(cell == side * half_cells + k, got, out)
                    made.append((ref, slot, to, 1 - side, out))
        for ref, slot, to, at, out in made:
            ref[*slot, to, at] = out

    def over(span, body):
        steps, count, entries = span
        if steps == 1:
            body(entries)
            return
        def one(i, carry):
            body([tuple(chosen(i, [entries[n * count + u][at] for n in range(steps)]) for at in (0, 1)) for u in range(count)])
            return carry
        lax.fori_loop(0, steps, one, 0)

    def items(entries):
        for offset, side in entries:
            d = domain_of(offset)
            for k in range(half_cells):
                lane = side * half_lanes + k * LANES
                yield d, lane if isinstance(lane, int) else pl.multiple_of(lane, LANES), k

    def ghost_rows(ref, slot, d, k):
        side, pair = divmod(k, 2)
        return [bcast(ref, (*slot, d, side), 2 * c + pair, 0) for c in range(3)]

    def blocks(d, lane):
        for g in range(groups):
            yield (d, slice(g * ROWS, (g + 1) * ROWS), pl.ds(lane, LANES))

    def total(block):
        for shift in (4, 2, 1):
            block = block + pltpu.roll(block, shift, 0)
        return block

    def force(level, sub, d, lane, k):
        mine = [bcast(state, (level, d), 2 * c, lane) for c in range(3)]
        far = ghost_rows(ghost, (), d, k)
        sums = [None] * 3
        for at in blocks(d, lane):
            entry = close[at]
            places = entry & (LANES - 1)
            near = entry < LANES
            delta = [m - jnp.where(near, lane_gather(m, places), lane_gather(f, places)) for m, f in zip(mine, far)]
            radius = delta[0] * delta[0] + delta[1] * delta[1] + delta[2] * delta[2] + short_core * short_core
            inverse = lax.rsqrt(radius)
            w = weight[(sub, *at)] * (inverse * inverse * inverse)
            for c in range(3):
                term = w * delta[c]
                sums[c] = term if sums[c] is None else sums[c] + term
        sums = [total(s) for s in sums]
        return jnp.where(x_rows, sums[0], jnp.where(y_rows, sums[1], sums[2]))

    def evaluate(level, owners, halves):
        sub = level // 2
        stage = lax.rem(level, 2)
        base = level - stage
        over(owners, lambda owners: owner_picks(owners, sub, ((state.at[level], ghost, ()),)))

        def one(entries):
            made = []
            for d, lane, k in items(entries):
                here = pl.ds(lane, LANES)
                vel = bcast(now, (d,), MOB, lane) * (long_[d, :, here] + force(level, sub, d, lane, k))
                vel = jnp.where(stage == 1, 0.5 * (vels[base, d, :, here] + vel), vel)
                made.append((d, here, vel, state[base, d, :, here] + time_step * vel))
            for d, here, vel, moved in made:
                vels[level, d, :, here] = vel
                state[level + 1, d, :, here] = moved

        over(halves, one)

    for first, last, owners, halves in plan["levels"]:
        if last - first == 1:
            evaluate(jnp.int32(first), owners, halves)
        else:
            lax.fori_loop(first, last, lambda level, carry: (evaluate(level, owners, halves), carry)[1], 0)

    for c in range(3):
        out_pos[c : c + 1, :] = state[evals, me, 2 * c : 2 * c + 1, :]
        out_vel[c : c + 1, :] = vels[evals - 1, me, 2 * c : 2 * c + 1, :]


def span(entries, limit):
    count = min(range(1, limit + 1), key=lambda c: (-(-len(entries) // c) * (c + 0.5), c))
    steps = -(-len(entries) // count)
    return steps, count, entries + [entries[-1]] * (steps * count - len(entries))


def chosen(step, values):
    if len(set(values)) == 1:
        return values[0]
    if [v - values[0] for v in values] == [n * (values[1] - values[0]) for n in range(len(values))]:
        return values[0] + step * (values[1] - values[0])
    out = values[-1]
    for n in range(len(values) - 2, -1, -1):
        out = jnp.where(step == n, values[n], out)
    return out


def owners_of(level, domains):
    return sorted({((d + s) % domains, 0) for d, _ in level for s in (1, -1)})


ANYWHERE = pl.BlockSpec(memory_space=pl.ANY)
VMEM = pl.BlockSpec(memory_space=pltpu.VMEM)


def pair_weights(blocks, slots, subs, own_index, most=2, most_owners=4):
    domains = len(blocks)
    rows, seg = blocks[0].shape
    levels = level_halves(domains, 2 * subs)
    plan = {"still": [span(owners_of(levels[2 * t], domains), most_owners) for t in range(subs)], "weights": []}
    for upto in range(1, subs + 1):
        after = levels[2 * upto] if upto < subs else []
        only = [h for h in levels[2 * upto - 2] if h not in after]
        if only:
            plan["weights"].append((upto, span(only, most)))

    def kernel(*refs):
        weights_kernel(domains, slots, subs, plan, own_index, *refs)

    return pl.pallas_call(
        kernel,
        out_shape=[
            jax.ShapeDtypeStruct((subs, domains, slots, seg), jnp.float32),
            jax.ShapeDtypeStruct((domains, slots, seg), jnp.int32),
            jax.ShapeDtypeStruct((domains, ROWS, seg), jnp.int32),
        ],
        in_specs=[ANYWHERE] * domains,
        out_specs=[VMEM] * 3,
        scratch_shapes=[
            pltpu.VMEM((domains, rows, seg), jnp.float32),
            pltpu.VMEM((2, domains, ROWS, seg), jnp.float32),
            pltpu.VMEM((subs, 2, domains, 2, ROWS, LANES), jnp.float32),
            pltpu.SemaphoreType.DMA((domains,)),
        ],
        compiler_params=pltpu.CompilerParams(vmem_limit_bytes=WEIGHT_VMEM * 2**20),
        cost_estimate=pl.CostEstimate(flops=10**7, bytes_accessed=4 * 10**7, transcendentals=0),
        name="weights",
    )(*blocks)


def step(now, weights, subs, own_index, most=8, most_owners=8):
    domains = len(now)
    rows, seg = now[0].shape
    slots = weights[0].shape[2]
    levels = level_halves(domains, 2 * subs)
    plan = {"levels": []}
    first = 0
    while first < len(levels):
        last = first + 1
        while last < len(levels) and levels[last] == levels[first]:
            last += 1
        plan["levels"].append((first, last, span(owners_of(levels[first], domains), most_owners), span(levels[first], most)))
        first = last

    def kernel(*refs):
        step_kernel(domains, slots, subs, plan, own_index, *refs)

    return pl.pallas_call(
        kernel,
        out_shape=[jax.ShapeDtypeStruct((3, seg), jnp.float32)] * 2,
        in_specs=[ANYWHERE] * domains + [VMEM] * 3,
        out_specs=[VMEM] * 2,
        scratch_shapes=[
            pltpu.VMEM((domains, rows, seg), jnp.float32),
            pltpu.VMEM((2 * subs + 1, domains, ROWS, seg), jnp.float32),
            pltpu.VMEM((2 * subs, domains, ROWS, seg), jnp.float32),
            pltpu.VMEM((domains, ROWS, seg), jnp.float32),
            pltpu.VMEM((domains, 2, ROWS, LANES), jnp.float32),
            pltpu.SemaphoreType.DMA((domains,)),
        ],
        compiler_params=pltpu.CompilerParams(vmem_limit_bytes=STEP_VMEM * 2**20),
        cost_estimate=pl.CostEstimate(flops=10**7, bytes_accessed=6 * 10**7, transcendentals=10**6),
        name="step",
    )(*now, *weights)


def pack_kernel(*refs):
    here, (block, state), held, sem = refs[:6], refs[6:8], refs[8:14], refs[14]
    copies = [pltpu.make_async_copy(src, dst, sem.at[n]) for n, (src, dst) in enumerate(zip(here, held))]
    for copy in copies:
        copy.start()
    for copy in copies:
        copy.wait()
    positions, line_vectors, burgers, mobility, close_list, ghost_map = held
    slots, seg = close_list.shape
    block[:slots, :] = close_list[...].astype(jnp.float32)
    state[0:3, :] = positions[...]
    for at, ref in ((0, line_vectors), (3, burgers)):
        block[slots + at : slots + at + 3, :] = ref[...]
        state[3 + at : 6 + at, :] = ref[...]
    state[9:10, :] = mobility[...]
    subs, wide = ghost_map.shape
    per = seg // wide
    for t in range(subs):
        at = slots + 6 + t // per
        block[at : at + 1, (t % per) * wide : (t % per + 1) * wide] = ghost_map[t : t + 1, :].astype(jnp.float32)


def packed(*arrays):
    slots, seg = arrays[4].shape
    return pl.pallas_call(
        pack_kernel,
        out_shape=[jax.ShapeDtypeStruct((slots + 6 + arrays[5].size // seg, seg), jnp.float32), jax.ShapeDtypeStruct((10, seg), jnp.float32)],
        in_specs=[pl.BlockSpec(memory_space=pltpu.HBM)] * 6,
        out_specs=[VMEM] * 2,
        scratch_shapes=[pltpu.VMEM(a.shape, a.dtype) for a in arrays] + [pltpu.SemaphoreType.DMA((6,))],
        compiler_params=pltpu.CompilerParams(vmem_limit_bytes=PACK_VMEM * 2**20),
        name="pack",
    )(*arrays)


def split(rows):
    parts = []
    for _ in range(3):
        parts.append(rows.astype(jnp.bfloat16).astype(jnp.float32))
        rows = rows - parts[-1]
    return parts


SOURCE_PARTS = (0, 0, 1, 0, 2, 1)
TARGET_PARTS = (0, 1, 0, 2, 0, 1)
FEATURES = 48


def long_kernel(sources, seg, unroll, *refs):
    states, block = refs[: sources + 1], refs[sources + 1]
    out, held, features, aims, sem = refs[sources + 2 :]
    copy = pltpu.make_async_copy(block, held, sem)
    copy.start()
    cells = seg // LANES
    scale = 1.0 / math.sqrt((sources + 1) * LANES)
    zero = jnp.zeros((3, seg), jnp.float32)
    for s in range(sources + 1):
        vectors = (states[s][3:6, :], states[s][6:9, :])
        for n, vector in enumerate(vectors):
            parts = split(vector)
            for k, part in enumerate(SOURCE_PARTS):
                features[s, 18 * n + 3 * k : 18 * n + 3 * k + 3, :] = parts[part]
            if s == 0:
                for k, part in enumerate(TARGET_PARTS):
                    aims[18 * n + 3 * k : 18 * n + 3 * k + 3, :] = parts[part]
        for k, part in enumerate(split(states[s][0:3, :])):
            features[s, 36 + 3 * k : 39 + 3 * k, :] = part
        features[s, 45:48, :] = zero
    out[0:3, :] = states[0][0:3, :]
    out[3:4, :] = states[0][9:10, :]
    row = lax.broadcasted_iota(jnp.int32, (FEATURES, LANES), 0)
    column_of = [jnp.where((row >= 36) & (row < 45) & (row % 3 == c), 1.0, 0.0) for c in range(3)]

    def cell_at(lane):
        here = pl.ds(lane, LANES)
        aim = aims[:, here]
        right = jnp.concatenate([jnp.where(row < 18, aim, 0.0), jnp.where((row >= 18) & (row < 36), aim, 0.0), *column_of], 1).astype(jnp.bfloat16)
        mine = [states[0][c : c + 1, here] for c in range(3)]
        forces = [jnp.zeros((ROWS, LANES), jnp.float32)] * 3
        for s in range(sources + 1):
            left = jnp.transpose(features[s, :, here]).astype(jnp.bfloat16)
            made = jnp.dot(left, right, preferred_element_type=jnp.float32)
            line, burg, *at = [made[:, n * LANES : (n + 1) * LANES] for n in range(5)]
            delta = [m - a for m, a in zip(mine, at)]
            radius = delta[0] * delta[0] + delta[1] * delta[1] + delta[2] * delta[2] + long_core * long_core
            inverse = lax.rsqrt(radius)
            w = burg * line * (inverse * inverse * inverse)
            for c in range(3):
                forces[c] = forces[c] + jnp.sum((w * delta[c]).reshape(-1, ROWS, LANES), 0)
        return [jnp.sum(f, 0, keepdims=True) * scale for f in forces]

    def one(i, carry):
        lanes = [pl.multiple_of((i * unroll + u) * LANES, LANES) for u in range(unroll)]
        made = [cell_at(lane) for lane in lanes]
        for lane, forces in zip(lanes, made):
            for c in range(3):
                out[4 + c : 5 + c, pl.ds(lane, LANES)] = forces[c]
        return carry

    aims[36:48, :] = jnp.zeros((12, seg), jnp.float32)
    lax.fori_loop(0, cells // unroll, one, 0)
    copy.wait()


def long_range(state, others, block, unroll=8):
    seg = state.shape[1]
    return pl.pallas_call(
        lambda *refs: long_kernel(len(others), seg, unroll, *refs),
        out_shape=[jax.ShapeDtypeStruct((ROWS, seg), jnp.float32), jax.ShapeDtypeStruct(block.shape, block.dtype)],
        in_specs=[VMEM] * (1 + len(others)) + [pl.BlockSpec(memory_space=pl.ANY)],
        out_specs=[VMEM] * 2,
        scratch_shapes=[pltpu.VMEM((len(others) + 1, FEATURES, seg), jnp.float32), pltpu.VMEM((FEATURES, seg), jnp.float32), pltpu.SemaphoreType.DMA(())],
        compiler_params=pltpu.CompilerParams(vmem_limit_bytes=SMALL_VMEM * 2**20),
        cost_estimate=pl.CostEstimate(flops=10**7, bytes_accessed=2 * 10**7, transcendentals=10**6),
        name="long_range",
    )(state, *others, block)


def shifted(value, axis, steps):
    count = lax.axis_size(axis)
    return lax.ppermute(value, axis, [(i, (i + steps) % count) for i in range(count)])


def matched(value, axis, step):
    count = lax.axis_size(axis)
    return lax.ppermute(value, axis, [(i, i ^ step) for i in range(count)])


def cycle_neighbours(value, axis):
    count = lax.axis_size(axis)
    got = [matched(value, axis, 1), lax.ppermute(value, axis, [(i, (((i - 1) % count) ^ 1) + 1 if ((i - 1) % count) ^ 1 != count - 1 else 0) for i in range(count)])]
    for k in range(2, count // 4 + 1):
        got += [shifted(value, axis, k), shifted(value, axis, -k)]
    return got


def local(positions, line_vectors, burgers, mobility, close_list, ghost_map):
    slots, seg = close_list.shape
    subs = ghost_map.shape[0]
    half = lax.axis_size("dom") // 2
    own_index = lambda: lax.axis_index("dom")
    block, state = packed(positions, line_vectors, burgers, mobility[None], close_list, ghost_map)
    others = cycle_neighbours(state, "blk")
    far_first = range(half - 1, 0, -1)
    blocks = [matched(block, "dom", 2 * j) for j in far_first[:3]]
    now, block = long_range(state, others, block)
    blocks, now = lax.optimization_barrier((blocks, now))
    nows = [now] + [matched(now, "dom", 2 * j) for j in range(1, half)]
    blocks = [block] + blocks
    blocks = blocks + [matched(b, "dom", 1) for b in blocks]
    weights = pair_weights(blocks, slots, subs, own_index)
    nows, weights = lax.optimization_barrier((nows, weights))
    nows = nows + [matched(n, "dom", 1) for n in nows]
    return tuple(step(nows, weights, subs, own_index))


def solution(mesh):
    spread = P(None, ("blk", "dom"))
    return jax.shard_map(
        local,
        mesh=mesh,
        in_specs=(spread, spread, spread, P(("blk", "dom")), spread, spread),
        out_specs=(spread, spread),
        check_vma=False,
    )
```

```python
import math

import jax
import jax.numpy as jnp
from jax import lax
from jax.experimental import pallas as pl
from jax.experimental.pallas import tpu as pltpu
from jax.sharding import PartitionSpec as P

LANES = 128
ROWS = 8
long_core = 1.0
short_core = 0.25
time_step = 0.05


def lane_gather(row_block, places):
    return jnp.take_along_axis(row_block, places, axis=1, mode="promise_in_bounds")


def level_halves(domains, evals):
    levels = [{(0, 0), (0, 1)}]
    for _ in range(evals - 1):
        last = levels[-1]
        grown = set(last)
        for domain in {d for d, _ in last}:
            grown.add(((domain - 1) % domains, 1))
            grown.add(((domain + 1) % domains, 0))
        levels.append(grown)
    return [sorted(level) for level in levels[::-1]]


EXPAND = 4
SMALL_VMEM = 8
PACK_VMEM = 60
WEIGHT_VMEM = 24
STEP_VMEM = 24

def fetch(refs, held, me, sem, order):
    half = held.shape[0] // 2
    copies = []
    for j in range(half):
        for other in range(2):
            at = other * half + j
            src = refs[at] if len(refs) > half else refs[j].at[pl.ds(other * held.shape[1], held.shape[1])]
            copies.append(pltpu.make_async_copy(src, held.at[me ^ (2 * order[j] + other)], sem.at[at]))
    for copy in copies:
        copy.start()
    for copy in copies:
        copy.wait()


def weights_kernel(domains, slots, subs, plan, own_index, *refs):
    block_refs = refs[:domains]
    weight, close, gplaces, pack, still_rows, still, sem = refs[domains:]
    seg = pack.shape[2]
    cells = seg // LANES
    groups = slots // ROWS
    half_cells = cells // 2
    half_lanes = half_cells * LANES
    ghosts = seg // (2 * (subs // 2))
    me = own_index()
    scale = 1.0 / math.sqrt(slots)
    LINE, BURG, GHOST = slots, slots + 3, slots + 6
    fetch(block_refs, pack, me, sem, [0, *range(domains // 2 - 1, 0, -1)])

    row = lax.broadcasted_iota(jnp.int32, (ROWS, LANES), 0)
    x_rows = row < 2
    y_rows = row < 4

    even_row = lax.rem(row, 2) == 0

    def bcast(ref, index, at, lane):
        return jnp.broadcast_to(ref[*index, at : at + 1, pl.ds(lane, LANES)], (ROWS, LANES))

    def spread(ref, d, at, lane):
        x, y, z = (bcast(ref, (d,), at + c, lane) for c in range(3))
        return jnp.where(x_rows, x, jnp.where(y_rows, y, z))

    def expand(d, carry):
        for q in range(cells):
            here = pl.ds(q * LANES, LANES)
            for at, slot in ((LINE, 0), (BURG, 1)):
                still_rows[slot, d, :, here] = spread(pack, d, at, q * LANES)
        for sub in range(subs):
            for side in range(2):
                lane = (sub % 2) * 2 * ghosts + side * ghosts
                at = GHOST + sub // 2
                place = jnp.where(even_row, bcast(pack, (d,), at, lane), bcast(pack, (d,), at, lane + LANES))
                gplaces[d, :, pl.ds((2 * sub + side) * LANES, LANES)] = place.astype(jnp.int32)
        return carry

    lax.fori_loop(0, domains, expand, 0, unroll=EXPAND)

    def domain_of(offset):
        return lax.rem(offset + me, domains)

    def owner_picks(owners, sub, sources):
        made = []
        for offset, _ in owners:
            d = domain_of(offset)
            for side in range(2):
                place = gplaces[d, :, pl.ds(pl.multiple_of((2 * sub + side) * LANES, LANES), LANES)]
                lane = place & (LANES - 1)
                cell = place >> 7
                to = lax.rem(d + (1 if side else domains - 1), domains)
                for source, ref, slot in sources:
                    out = None
                    for k in range(half_cells):
                        got = lane_gather(source[d, :, pl.ds(side * half_lanes + k * LANES, LANES)], lane)
                        out = got if out is None else jnp.where(cell == side * half_cells + k, got, out)
                    made.append((ref, slot, to, 1 - side, out))
        for ref, slot, to, at, out in made:
            ref[*slot, to, at] = out

    def over(span, body):
        steps, count, entries = span
        if steps == 1:
            body(entries)
            return
        def one(i, carry):
            body([tuple(chosen(i, [entries[n * count + u][at] for n in range(steps)]) for at in (0, 1)) for u in range(count)])
            return carry
        lax.fori_loop(0, steps, one, 0)

    def items(entries):
        for offset, side in entries:
            d = domain_of(offset)
            for k in range(half_cells):
                lane = side * half_lanes + k * LANES
                yield d, lane if isinstance(lane, int) else pl.multiple_of(lane, LANES), k

    def dots(mine, theirs):
        return mine[0] * theirs[0] + mine[1] * theirs[1] + mine[2] * theirs[2]

    def pair_weight(mine, source, places):
        theirs = [lane_gather(m, places) for m in source]
        return dots(mine[:3], theirs[:3]) * dots(mine[3:], theirs[3:]) * scale

    def ghost_rows(ref, slot, d, k):
        side, pair = divmod(k, 2)
        return [bcast(ref, (*slot, d, side), 2 * c + pair, 0) for c in range(3)]

    def blocks(d, lane):
        for g in range(groups):
            yield (d, slice(g * ROWS, (g + 1) * ROWS), pl.ds(lane, LANES))

    def weights(entries, upto):
        made = []
        for d, lane, k in items(entries):
            mine = [bcast(pack, (d,), LINE + c, lane) for c in range(6)]
            far = [ghost_rows(still, (sub, 0), d, k) + ghost_rows(still, (sub, 1), d, k) for sub in range(upto)]
            for at in blocks(d, lane):
                entry = pack[at].astype(jnp.int32)
                places = entry & (LANES - 1)
                near, held = entry < LANES, entry < 2 * LANES
                near_w = pair_weight(mine, mine, places)
                made.append((close.at[at], entry))
                for sub in range(upto):
                    made.append((weight.at[(sub, *at)], jnp.where(near, near_w, jnp.where(held, pair_weight(mine, far[sub], places), 0.0))))
        for ref, value in made:
            ref[...] = value

    for sub in range(subs):
        over(plan["still"][sub], lambda owners: owner_picks(owners, sub, ((still_rows.at[0], still, (sub, 0)), (still_rows.at[1], still, (sub, 1)))))
    for upto, span in plan["weights"]:
        over(span, lambda entries: weights(entries, upto))


def step_kernel(domains, slots, subs, plan, own_index, *refs):
    half = domains // 2
    now_refs = refs[:half]
    weight, close, gplaces = refs[half : half + 3]
    out_pos, out_vel = refs[half + 3 : half + 5]
    now, state, vels, long_, ghost, sem = refs[half + 5 :]
    seg = now.shape[2]
    evals = vels.shape[0]
    cells = seg // LANES
    groups = slots // ROWS
    half_cells = cells // 2
    half_lanes = half_cells * LANES
    me = own_index()
    POS, MOB, FAR = 0, 3, 4
    fetch(now_refs, now, me, sem, range(domains // 2))

    row = lax.broadcasted_iota(jnp.int32, (ROWS, LANES), 0)
    x_rows = row < 2
    y_rows = row < 4

    def bcast(ref, index, at, lane):
        return jnp.broadcast_to(ref[*index, at : at + 1, pl.ds(lane, LANES)], (ROWS, LANES))

    def spread(d, at, lane):
        x, y, z = (bcast(now, (d,), at + c, lane) for c in range(3))
        return jnp.where(x_rows, x, jnp.where(y_rows, y, z))

    def expand(d, carry):
        for q in range(cells):
            here = pl.ds(q * LANES, LANES)
            state[0, d, :, here] = spread(d, POS, q * LANES)
            long_[d, :, here] = spread(d, FAR, q * LANES)
        return carry

    lax.fori_loop(0, domains, expand, 0, unroll=EXPAND)

    def domain_of(offset):
        return lax.rem(offset + me, domains)

    def owner_picks(owners, sub, sources):
        made = []
        for offset, _ in owners:
            d = domain_of(offset)
            for side in range(2):
                place = gplaces[d, :, pl.ds(pl.multiple_of((2 * sub + side) * LANES, LANES), LANES)]
                lane = place & (LANES - 1)
                cell = place >> 7
                to = lax.rem(d + (1 if side else domains - 1), domains)
                for source, ref, slot in sources:
                    out = None
                    for k in range(half_cells):
                        got = lane_gather(source[d, :, pl.ds(side * half_lanes + k * LANES, LANES)], lane)
                        out = got if out is None else jnp.where(cell == side * half_cells + k, got, out)
                    made.append((ref, slot, to, 1 - side, out))
        for ref, slot, to, at, out in made:
            ref[*slot, to, at] = out

    def over(span, body):
        steps, count, entries = span
        if steps == 1:
            body(entries)
            return
        def one(i, carry):
            body([tuple(chosen(i, [entries[n * count + u][at] for n in range(steps)]) for at in (0, 1)) for u in range(count)])
            return carry
        lax.fori_loop(0, steps, one, 0)

    def items(entries):
        for offset, side in entries:
            d = domain_of(offset)
            for k in range(half_cells):
                lane = side * half_lanes + k * LANES
                yield d, lane if isinstance(lane, int) else pl.multiple_of(lane, LANES), k

    def ghost_rows(ref, slot, d, k):
        side, pair = divmod(k, 2)
        return [bcast(ref, (*slot, d, side), 2 * c + pair, 0) for c in range(3)]

    def blocks(d, lane):
        for g in range(groups):
            yield (d, slice(g * ROWS, (g + 1) * ROWS), pl.ds(lane, LANES))

    def total(block):
        for shift in (4, 2, 1):
            block = block + pltpu.roll(block, shift, 0)
        return block

    def force(level, sub, d, lane, k):
        mine = [bcast(state, (level, d), 2 * c, lane) for c in range(3)]
        far = ghost_rows(ghost, (), d, k)
        sums = [None] * 3
        for at in blocks(d, lane):
            entry = close[at]
            places = entry & (LANES - 1)
            near = entry < LANES
            delta = [m - jnp.where(near, lane_gather(m, places), lane_gather(f, places)) for m, f in zip(mine, far)]
            radius = delta[0] * delta[0] + delta[1] * delta[1] + delta[2] * delta[2] + short_core * short_core
            inverse = lax.rsqrt(radius)
            w = weight[(sub, *at)] * (inverse * inverse * inverse)
            for c in range(3):
                term = w * delta[c]
                sums[c] = term if sums[c] is None else sums[c] + term
        sums = [total(s) for s in sums]
        return jnp.where(x_rows, sums[0], jnp.where(y_rows, sums[1], sums[2]))

    def evaluate(level, owners, halves):
        sub = level // 2
        stage = lax.rem(level, 2)
        base = level - stage
        over(owners, lambda owners: owner_picks(owners, sub, ((state.at[level], ghost, ()),)))

        def one(entries):
            made = []
            for d, lane, k in items(entries):
                here = pl.ds(lane, LANES)
                vel = bcast(now, (d,), MOB, lane) * (long_[d, :, here] + force(level, sub, d, lane, k))
                vel = jnp.where(stage == 1, 0.5 * (vels[base, d, :, here] + vel), vel)
                made.append((d, here, vel, state[base, d, :, here] + time_step * vel))
            for d, here, vel, moved in made:
                vels[level, d, :, here] = vel
                state[level + 1, d, :, here] = moved

        over(halves, one)

    for first, last, owners, halves in plan["levels"]:
        if last - first == 1:
            evaluate(jnp.int32(first), owners, halves)
        else:
            lax.fori_loop(first, last, lambda level, carry: (evaluate(level, owners, halves), carry)[1], 0)

    for c in range(3):
        out_pos[c : c + 1, :] = state[evals, me, 2 * c : 2 * c + 1, :]
        out_vel[c : c + 1, :] = vels[evals - 1, me, 2 * c : 2 * c + 1, :]


def span(entries, limit):
    count = min(range(1, limit + 1), key=lambda c: (-(-len(entries) // c) * (c + 0.5), c))
    steps = -(-len(entries) // count)
    return steps, count, entries + [entries[-1]] * (steps * count - len(entries))


def chosen(step, values):
    if len(set(values)) == 1:
        return values[0]
    if [v - values[0] for v in values] == [n * (values[1] - values[0]) for n in range(len(values))]:
        return values[0] + step * (values[1] - values[0])
    out = values[-1]
    for n in range(len(values) - 2, -1, -1):
        out = jnp.where(step == n, values[n], out)
    return out


def owners_of(level, domains):
    return sorted({((d + s) % domains, 0) for d, _ in level for s in (1, -1)})


ANYWHERE = pl.BlockSpec(memory_space=pl.ANY)
VMEM = pl.BlockSpec(memory_space=pltpu.VMEM)


def pair_weights(blocks, slots, subs, own_index, most=4, most_owners=8):
    domains = len(blocks)
    rows, seg = blocks[0].shape
    levels = level_halves(domains, 2 * subs)
    plan = {"still": [span(owners_of(levels[2 * t], domains), most_owners) for t in range(subs)], "weights": []}
    for upto in range(1, subs + 1):
        after = levels[2 * upto] if upto < subs else []
        only = [h for h in levels[2 * upto - 2] if h not in after]
        if only:
            plan["weights"].append((upto, span(only, most)))

    def kernel(*refs):
        weights_kernel(domains, slots, subs, plan, own_index, *refs)

    return pl.pallas_call(
        kernel,
        out_shape=[
            jax.ShapeDtypeStruct((subs, domains, slots, seg), jnp.float32),
            jax.ShapeDtypeStruct((domains, slots, seg), jnp.int32),
            jax.ShapeDtypeStruct((domains, ROWS, seg), jnp.int32),
        ],
        in_specs=[ANYWHERE] * domains,
        out_specs=[VMEM] * 3,
        scratch_shapes=[
            pltpu.VMEM((domains, rows, seg), jnp.float32),
            pltpu.VMEM((2, domains, ROWS, seg), jnp.float32),
            pltpu.VMEM((subs, 2, domains, 2, ROWS, LANES), jnp.float32),
            pltpu.SemaphoreType.DMA((domains,)),
        ],
        compiler_params=pltpu.CompilerParams(vmem_limit_bytes=WEIGHT_VMEM * 2**20),
        cost_estimate=pl.CostEstimate(flops=10**7, bytes_accessed=4 * 10**7, transcendentals=0),
        name="weights",
    )(*blocks)


def step(now, weights, subs, own_index, most=16, most_owners=8):
    domains = 2 * len(now)
    rows, seg = now[0].shape[0] // 2, now[0].shape[1]
    slots = weights[0].shape[2]
    levels = level_halves(domains, 2 * subs)
    plan = {"levels": []}
    first = 0
    while first < len(levels):
        last = first + 1
        while last < len(levels) and levels[last] == levels[first]:
            last += 1
        plan["levels"].append((first, last, span(owners_of(levels[first], domains), most_owners), span(levels[first], most)))
        first = last

    def kernel(*refs):
        step_kernel(domains, slots, subs, plan, own_index, *refs)

    return pl.pallas_call(
        kernel,
        out_shape=[jax.ShapeDtypeStruct((3, seg), jnp.float32)] * 2,
        in_specs=[ANYWHERE] * len(now) + [VMEM] * 3,
        out_specs=[VMEM] * 2,
        scratch_shapes=[
            pltpu.VMEM((domains, rows, seg), jnp.float32),
            pltpu.VMEM((2 * subs + 1, domains, ROWS, seg), jnp.float32),
            pltpu.VMEM((2 * subs, domains, ROWS, seg), jnp.float32),
            pltpu.VMEM((domains, ROWS, seg), jnp.float32),
            pltpu.VMEM((domains, 2, ROWS, LANES), jnp.float32),
            pltpu.SemaphoreType.DMA((domains,)),
        ],
        compiler_params=pltpu.CompilerParams(vmem_limit_bytes=STEP_VMEM * 2**20),
        cost_estimate=pl.CostEstimate(flops=10**7, bytes_accessed=6 * 10**7, transcendentals=10**6),
        name="step",
    )(*now, *weights)


def pack_kernel(*refs):
    here, block, held, sem = refs[:4], refs[4], refs[5:9], refs[9]
    copies = [pltpu.make_async_copy(src, dst, sem.at[n]) for n, (src, dst) in enumerate(zip(here, held))]
    for copy in copies:
        copy.start()
    for copy in copies:
        copy.wait()
    line_vectors, burgers, close_list, ghost_map = held
    slots, seg = close_list.shape
    block[:slots, :] = close_list[...].astype(jnp.float32)
    block[slots : slots + 3, :] = line_vectors[...]
    block[slots + 3 : slots + 6, :] = burgers[...]
    subs, wide = ghost_map.shape
    per = seg // wide
    for t in range(subs):
        at = slots + 6 + t // per
        block[at : at + 1, (t % per) * wide : (t % per + 1) * wide] = ghost_map[t : t + 1, :].astype(jnp.float32)


def packed(*arrays):
    slots, seg = arrays[2].shape
    return pl.pallas_call(
        pack_kernel,
        out_shape=jax.ShapeDtypeStruct((slots + 6 + arrays[3].size // seg, seg), jnp.float32),
        in_specs=[pl.BlockSpec(memory_space=pl.ANY)] * len(arrays),
        out_specs=VMEM,
        scratch_shapes=[pltpu.VMEM(a.shape, a.dtype) for a in arrays] + [pltpu.SemaphoreType.DMA((len(arrays),))],
        compiler_params=pltpu.CompilerParams(vmem_limit_bytes=PACK_VMEM * 2**20),
        name="pack",
    )(*arrays)


def split(rows):
    parts = []
    for _ in range(3):
        parts.append(rows.astype(jnp.bfloat16).astype(jnp.float32))
        rows = rows - parts[-1]
    return parts


SOURCE_PARTS = (0, 0, 1, 0, 2, 1)
TARGET_PARTS = (0, 1, 0, 2, 0, 1)
FEATURES = 48


def long_kernel(sources, seg, unroll, *refs):
    states, block = refs[: sources + 1], refs[sources + 1]
    out, held, features, aims, sem = refs[sources + 2 :]
    copy = pltpu.make_async_copy(block, held, sem)
    copy.start()
    cells = seg // LANES
    scale = 1.0 / math.sqrt((sources + 1) * LANES)
    zero = jnp.zeros((3, seg), jnp.float32)
    for s in range(sources + 1):
        vectors = (states[s][3:6, :], states[s][6:9, :])
        for n, vector in enumerate(vectors):
            parts = split(vector)
            for k, part in enumerate(SOURCE_PARTS):
                features[s, 18 * n + 3 * k : 18 * n + 3 * k + 3, :] = parts[part]
            if s == 0:
                for k, part in enumerate(TARGET_PARTS):
                    aims[18 * n + 3 * k : 18 * n + 3 * k + 3, :] = parts[part]
        for k, part in enumerate(split(states[s][0:3, :])):
            features[s, 36 + 3 * k : 39 + 3 * k, :] = part
        features[s, 45:48, :] = zero
    out[0:3, :] = states[0][0:3, :]
    out[3:4, :] = states[0][9:10, :]
    row = lax.broadcasted_iota(jnp.int32, (FEATURES, LANES), 0)
    column_of = [jnp.where((row >= 36) & (row < 45) & (row % 3 == c), 1.0, 0.0) for c in range(3)]

    def cell_at(lane):
        here = pl.ds(lane, LANES)
        aim = aims[:, here]
        right = jnp.concatenate([jnp.where(row < 18, aim, 0.0), jnp.where((row >= 18) & (row < 36), aim, 0.0), *column_of], 1).astype(jnp.bfloat16)
        mine = [states[0][c : c + 1, here] for c in range(3)]
        forces = [jnp.zeros((ROWS, LANES), jnp.float32)] * 3
        for s in range(sources + 1):
            left = jnp.transpose(features[s, :, here]).astype(jnp.bfloat16)
            made = jnp.dot(left, right, preferred_element_type=jnp.float32)
            line, burg, *at = [made[:, n * LANES : (n + 1) * LANES] for n in range(5)]
            delta = [m - a for m, a in zip(mine, at)]
            radius = delta[0] * delta[0] + delta[1] * delta[1] + delta[2] * delta[2] + long_core * long_core
            inverse = lax.rsqrt(radius)
            w = burg * line * (inverse * inverse * inverse)
            for c in range(3):
                forces[c] = forces[c] + jnp.sum((w * delta[c]).reshape(-1, ROWS, LANES), 0)
        return [jnp.sum(f, 0, keepdims=True) * scale for f in forces]

    def one(i, carry):
        lanes = [pl.multiple_of((i * unroll + u) * LANES, LANES) for u in range(unroll)]
        made = [cell_at(lane) for lane in lanes]
        for lane, forces in zip(lanes, made):
            for c in range(3):
                out[4 + c : 5 + c, pl.ds(lane, LANES)] = forces[c]
        return carry

    aims[36:48, :] = jnp.zeros((12, seg), jnp.float32)
    lax.fori_loop(0, cells // unroll, one, 0)
    copy.wait()


def long_range(state, others, block, unroll=8):
    seg = state.shape[1]
    return pl.pallas_call(
        lambda *refs: long_kernel(len(others), seg, unroll, *refs),
        out_shape=[jax.ShapeDtypeStruct((ROWS, seg), jnp.float32), jax.ShapeDtypeStruct(block.shape, block.dtype)],
        in_specs=[VMEM] * (1 + len(others)) + [pl.BlockSpec(memory_space=pl.ANY)],
        out_specs=[VMEM] * 2,
        scratch_shapes=[pltpu.VMEM((len(others) + 1, FEATURES, seg), jnp.float32), pltpu.VMEM((FEATURES, seg), jnp.float32), pltpu.SemaphoreType.DMA(())],
        compiler_params=pltpu.CompilerParams(vmem_limit_bytes=SMALL_VMEM * 2**20),
        cost_estimate=pl.CostEstimate(flops=10**7, bytes_accessed=2 * 10**7, transcendentals=10**6),
        name="long_range",
    )(state, *others, block)


def shifted(value, axis, steps):
    count = lax.axis_size(axis)
    return lax.ppermute(value, axis, [(i, (i + steps) % count) for i in range(count)])


def matched(value, axis, step):
    count = lax.axis_size(axis)
    return lax.ppermute(value, axis, [(i, i ^ step) for i in range(count)])


def cycle_neighbours(value, axis):
    count = lax.axis_size(axis)
    got = [matched(value, axis, 1), lax.ppermute(value, axis, [(i, (((i - 1) % count) ^ 1) + 1 if ((i - 1) % count) ^ 1 != count - 1 else 0) for i in range(count)])]
    for k in range(2, count // 4 + 1):
        got += [shifted(value, axis, k), shifted(value, axis, -k)]
    return got


def local(positions, line_vectors, burgers, mobility, close_list, ghost_map):
    slots, seg = close_list.shape
    subs = ghost_map.shape[0]
    half = lax.axis_size("dom") // 2
    own_index = lambda: lax.axis_index("dom")
    block = packed(line_vectors, burgers, close_list, ghost_map)
    state = jnp.concatenate([positions, line_vectors, burgers, mobility[None]], 0)
    others = cycle_neighbours(state, "blk")
    far_first = range(half - 1, 0, -1)
    blocks = [matched(block, "dom", 2 * j) for j in far_first[:3]]
    now, block = long_range(state, others, block)
    pair = jnp.concatenate([now, matched(now, "dom", 1)], 0)
    blocks, _ = lax.optimization_barrier((blocks, now))
    now = pair
    nows = [now] + [matched(now, "dom", 2 * j) for j in range(1, half)]
    blocks = [block] + blocks
    blocks = blocks + [matched(b, "dom", 1) for b in blocks]
    weights = pair_weights(blocks, slots, subs, own_index)
    nows, weights = lax.optimization_barrier((nows, weights))
    return tuple(step(nows, weights, subs, own_index))


def solution(mesh):
    spread = P(None, ("blk", "dom"))
    return jax.shard_map(
        local,
        mesh=mesh,
        in_specs=(spread, spread, spread, P(("blk", "dom")), spread, spread),
        out_specs=(spread, spread),
        check_vma=False,
    )
```

```python
import math

import jax
import jax.numpy as jnp
from jax import lax
from jax.experimental import pallas as pl
from jax.experimental.pallas import tpu as pltpu
from jax.sharding import PartitionSpec as P

LANES = 128
ROWS = 8
long_core = 1.0
short_core = 0.25
time_step = 0.05


def lane_gather(row_block, places):
    return jnp.take_along_axis(row_block, places, axis=1, mode="promise_in_bounds")


def level_halves(domains, evals):
    levels = [{(0, 0), (0, 1)}]
    for _ in range(evals - 1):
        last = levels[-1]
        grown = set(last)
        for domain in {d for d, _ in last}:
            grown.add(((domain - 1) % domains, 1))
            grown.add(((domain + 1) % domains, 0))
        levels.append(grown)
    return [sorted(level) for level in levels[::-1]]


EXPAND = 4
SMALL_VMEM = 8
PACK_VMEM = 60
WEIGHT_VMEM = 24
STEP_VMEM = 24

def fetch(refs, held, me, sem, order):
    half = held.shape[0] // 2
    copies = []
    for j in range(half):
        for other in range(2):
            at = other * half + j
            src = refs[at] if len(refs) > half else refs[j].at[pl.ds(other * held.shape[1], held.shape[1])]
            place = lax.rem((me ^ (2 * order[j] + other)) - me + 2 * half, 2 * half)
            copies.append(pltpu.make_async_copy(src, held.at[place], sem.at[at]))
    for copy in copies:
        copy.start()
    for copy in copies:
        copy.wait()


def weights_kernel(domains, slots, subs, plan, own_index, *refs):
    block_refs = refs[:domains]
    weight, close, gplaces, pack, still_rows, still, sem = refs[domains:]
    seg = pack.shape[2]
    cells = seg // LANES
    groups = slots // ROWS
    half_cells = cells // 2
    half_lanes = half_cells * LANES
    ghosts = seg // (2 * (subs // 2))
    me = own_index()
    scale = 1.0 / math.sqrt(slots)
    LINE, BURG, GHOST = slots, slots + 3, slots + 6
    fetch(block_refs, pack, me, sem, [0, *range(domains // 2 - 1, 0, -1)])

    row = lax.broadcasted_iota(jnp.int32, (ROWS, LANES), 0)
    x_rows = row < 2
    y_rows = row < 4

    even_row = lax.rem(row, 2) == 0

    def bcast(ref, index, at, lane):
        return jnp.broadcast_to(ref[*index, at : at + 1, pl.ds(lane, LANES)], (ROWS, LANES))

    def spread(ref, d, at, lane):
        x, y, z = (bcast(ref, (d,), at + c, lane) for c in range(3))
        return jnp.where(x_rows, x, jnp.where(y_rows, y, z))

    def expand(d, carry):
        for q in range(cells):
            here = pl.ds(q * LANES, LANES)
            for at, slot in ((LINE, 0), (BURG, 1)):
                still_rows[slot, d, :, here] = spread(pack, d, at, q * LANES)
        for sub in range(subs):
            for side in range(2):
                lane = (sub % 2) * 2 * ghosts + side * ghosts
                at = GHOST + sub // 2
                place = jnp.where(even_row, bcast(pack, (d,), at, lane), bcast(pack, (d,), at, lane + LANES))
                gplaces[d, :, pl.ds((2 * sub + side) * LANES, LANES)] = place.astype(jnp.int32)
        return carry

    lax.fori_loop(0, domains, expand, 0, unroll=EXPAND)

    def owner_picks(owners, sub, sources):
        made = []
        for offset, _ in owners:
            d = offset
            for side in range(2):
                place = gplaces[d, :, pl.ds(pl.multiple_of((2 * sub + side) * LANES, LANES), LANES)]
                lane = place & (LANES - 1)
                cell = place >> 7
                to = (d + (1 if side else domains - 1)) % domains
                for source, ref, slot in sources:
                    out = None
                    for k in range(half_cells):
                        got = lane_gather(source[d, :, pl.ds(side * half_lanes + k * LANES, LANES)], lane)
                        out = got if out is None else jnp.where(cell == side * half_cells + k, got, out)
                    made.append((ref, slot, to, 1 - side, out))
        for ref, slot, to, at, out in made:
            ref[*slot, to, at] = out

    def over(span, body):
        steps, count, entries = span
        if steps == 1:
            body(entries)
            return
        def one(i, carry):
            body([tuple(chosen(i, [entries[n * count + u][at] for n in range(steps)]) for at in (0, 1)) for u in range(count)])
            return carry
        lax.fori_loop(0, steps, one, 0)

    def items(entries):
        for offset, side in entries:
            d = offset
            for k in range(half_cells):
                lane = side * half_lanes + k * LANES
                yield d, lane if isinstance(lane, int) else pl.multiple_of(lane, LANES), k

    def dots(mine, theirs):
        return mine[0] * theirs[0] + mine[1] * theirs[1] + mine[2] * theirs[2]

    def pair_weight(mine, source, places):
        theirs = [lane_gather(m, places) for m in source]
        return dots(mine[:3], theirs[:3]) * dots(mine[3:], theirs[3:]) * scale

    def ghost_rows(ref, slot, d, k):
        side, pair = divmod(k, 2)
        return [bcast(ref, (*slot, d, side), 2 * c + pair, 0) for c in range(3)]

    def blocks(d, lane):
        for g in range(groups):
            yield (d, slice(g * ROWS, (g + 1) * ROWS), pl.ds(lane, LANES))

    def weights(entries, upto):
        made = []
        for d, lane, k in items(entries):
            mine = [bcast(pack, (d,), LINE + c, lane) for c in range(6)]
            far = [ghost_rows(still, (sub, 0), d, k) + ghost_rows(still, (sub, 1), d, k) for sub in range(upto)]
            for at in blocks(d, lane):
                entry = pack[at].astype(jnp.int32)
                places = entry & (LANES - 1)
                near, held = entry < LANES, entry < 2 * LANES
                near_w = pair_weight(mine, mine, places)
                made.append((close.at[at], entry))
                for sub in range(upto):
                    made.append((weight.at[(sub, *at)], jnp.where(near, near_w, jnp.where(held, pair_weight(mine, far[sub], places), 0.0))))
        for ref, value in made:
            ref[...] = value

    for sub in range(subs):
        over(plan["still"][sub], lambda owners: owner_picks(owners, sub, ((still_rows.at[0], still, (sub, 0)), (still_rows.at[1], still, (sub, 1)))))
    for upto, span in plan["weights"]:
        over(span, lambda entries: weights(entries, upto))


def step_kernel(domains, slots, subs, plan, own_index, *refs):
    half = domains // 2
    now_refs = refs[:half]
    weight, close, gplaces = refs[half : half + 3]
    out_pos, out_vel = refs[half + 3 : half + 5]
    now, state, vels, long_, ghost, sem = refs[half + 5 :]
    seg = now.shape[2]
    evals = vels.shape[0]
    cells = seg // LANES
    groups = slots // ROWS
    half_cells = cells // 2
    half_lanes = half_cells * LANES
    me = own_index()
    POS, MOB, FAR = 0, 3, 4
    fetch(now_refs, now, me, sem, range(domains // 2))

    row = lax.broadcasted_iota(jnp.int32, (ROWS, LANES), 0)
    x_rows = row < 2
    y_rows = row < 4

    def bcast(ref, index, at, lane):
        return jnp.broadcast_to(ref[*index, at : at + 1, pl.ds(lane, LANES)], (ROWS, LANES))

    def spread(d, at, lane):
        x, y, z = (bcast(now, (d,), at + c, lane) for c in range(3))
        return jnp.where(x_rows, x, jnp.where(y_rows, y, z))

    def expand(d, carry):
        for q in range(cells):
            here = pl.ds(q * LANES, LANES)
            state[0, d, :, here] = spread(d, POS, q * LANES)
            long_[d, :, here] = spread(d, FAR, q * LANES)
        return carry

    lax.fori_loop(0, domains, expand, 0, unroll=EXPAND)

    def owner_picks(owners, sub, sources):
        made = []
        for offset, _ in owners:
            d = offset
            for side in range(2):
                place = gplaces[d, :, pl.ds(pl.multiple_of((2 * sub + side) * LANES, LANES), LANES)]
                lane = place & (LANES - 1)
                cell = place >> 7
                to = (d + (1 if side else domains - 1)) % domains
                for source, ref, slot in sources:
                    out = None
                    for k in range(half_cells):
                        got = lane_gather(source[d, :, pl.ds(side * half_lanes + k * LANES, LANES)], lane)
                        out = got if out is None else jnp.where(cell == side * half_cells + k, got, out)
                    made.append((ref, slot, to, 1 - side, out))
        for ref, slot, to, at, out in made:
            ref[*slot, to, at] = out

    def over(span, body):
        steps, count, entries = span
        if steps == 1:
            body(entries)
            return
        def one(i, carry):
            body([tuple(chosen(i, [entries[n * count + u][at] for n in range(steps)]) for at in (0, 1)) for u in range(count)])
            return carry
        lax.fori_loop(0, steps, one, 0)

    def items(entries):
        for offset, side in entries:
            d = offset
            for k in range(half_cells):
                lane = side * half_lanes + k * LANES
                yield d, lane if isinstance(lane, int) else pl.multiple_of(lane, LANES), k

    def ghost_rows(ref, slot, d, k):
        side, pair = divmod(k, 2)
        return [bcast(ref, (*slot, d, side), 2 * c + pair, 0) for c in range(3)]

    def blocks(d, lane):
        for g in range(groups):
            yield (d, slice(g * ROWS, (g + 1) * ROWS), pl.ds(lane, LANES))

    def total(block):
        for shift in (4, 2, 1):
            block = block + pltpu.roll(block, shift, 0)
        return block

    def force(level, sub, d, lane, k):
        mine = [bcast(state, (level, d), 2 * c, lane) for c in range(3)]
        far = ghost_rows(ghost, (), d, k)
        sums = [None] * 3
        for at in blocks(d, lane):
            entry = close[at]
            places = entry & (LANES - 1)
            near = entry < LANES
            delta = [m - jnp.where(near, lane_gather(m, places), lane_gather(f, places)) for m, f in zip(mine, far)]
            radius = delta[0] * delta[0] + delta[1] * delta[1] + delta[2] * delta[2] + short_core * short_core
            inverse = lax.rsqrt(radius)
            w = weight[(sub, *at)] * (inverse * inverse * inverse)
            for c in range(3):
                term = w * delta[c]
                sums[c] = term if sums[c] is None else sums[c] + term
        sums = [total(s) for s in sums]
        return jnp.where(x_rows, sums[0], jnp.where(y_rows, sums[1], sums[2]))

    def evaluate(level, owners, halves):
        sub = level // 2
        stage = level % 2
        base = level - stage
        over(owners, lambda owners: owner_picks(owners, sub, ((state.at[level], ghost, ()),)))

        def one(entries):
            made = []
            for d, lane, k in items(entries):
                here = pl.ds(lane, LANES)
                vel = bcast(now, (d,), MOB, lane) * (long_[d, :, here] + force(level, sub, d, lane, k))
                if stage == 1:
                    vel = 0.5 * (vels[base, d, :, here] + vel)
                made.append((d, here, vel, state[base, d, :, here] + time_step * vel))
            for d, here, vel, moved in made:
                vels[level, d, :, here] = vel
                state[level + 1, d, :, here] = moved

        over(halves, one)

    for first, last, owners, halves in plan["levels"]:
        if last - first == 1:
            evaluate(first, owners, halves)
        else:
            lax.fori_loop(first, last, lambda level, carry: (evaluate(level, owners, halves), carry)[1], 0)

    for c in range(3):
        out_pos[c : c + 1, :] = state[evals, 0, 2 * c : 2 * c + 1, :]
        out_vel[c : c + 1, :] = vels[evals - 1, 0, 2 * c : 2 * c + 1, :]


def span(entries, limit):
    count = min(range(1, limit + 1), key=lambda c: (-(-len(entries) // c) * (c + 0.5), c))
    steps = -(-len(entries) // count)
    return steps, count, entries + [entries[-1]] * (steps * count - len(entries))


def chosen(step, values):
    if len(set(values)) == 1:
        return values[0]
    if [v - values[0] for v in values] == [n * (values[1] - values[0]) for n in range(len(values))]:
        return values[0] + step * (values[1] - values[0])
    out = values[-1]
    for n in range(len(values) - 2, -1, -1):
        out = jnp.where(step == n, values[n], out)
    return out


def owners_of(level, domains):
    return sorted({((d + s) % domains, 0) for d, _ in level for s in (1, -1)})


ANYWHERE = pl.BlockSpec(memory_space=pl.ANY)
VMEM = pl.BlockSpec(memory_space=pltpu.VMEM)


def pair_weights(blocks, slots, subs, own_index, most=4, most_owners=8):
    domains = len(blocks)
    rows, seg = blocks[0].shape
    levels = level_halves(domains, 2 * subs)
    plan = {"still": [span(owners_of(levels[2 * t], domains), most_owners) for t in range(subs)], "weights": []}
    for upto in range(1, subs + 1):
        after = levels[2 * upto] if upto < subs else []
        only = [h for h in levels[2 * upto - 2] if h not in after]
        if only:
            plan["weights"].append((upto, span(only, most)))

    def kernel(*refs):
        weights_kernel(domains, slots, subs, plan, own_index, *refs)

    return pl.pallas_call(
        kernel,
        out_shape=[
            jax.ShapeDtypeStruct((subs, domains, slots, seg), jnp.float32),
            jax.ShapeDtypeStruct((domains, slots, seg), jnp.int32),
            jax.ShapeDtypeStruct((domains, ROWS, seg), jnp.int32),
        ],
        in_specs=[ANYWHERE] * domains,
        out_specs=[VMEM] * 3,
        scratch_shapes=[
            pltpu.VMEM((domains, rows, seg), jnp.float32),
            pltpu.VMEM((2, domains, ROWS, seg), jnp.float32),
            pltpu.VMEM((subs, 2, domains, 2, ROWS, LANES), jnp.float32),
            pltpu.SemaphoreType.DMA((domains,)),
        ],
        compiler_params=pltpu.CompilerParams(vmem_limit_bytes=WEIGHT_VMEM * 2**20),
        cost_estimate=pl.CostEstimate(flops=10**7, bytes_accessed=4 * 10**7, transcendentals=0),
        name="weights",
    )(*blocks)


def step(now, weights, subs, own_index, most=16, most_owners=8):
    domains = 2 * len(now)
    rows, seg = now[0].shape[0] // 2, now[0].shape[1]
    slots = weights[0].shape[2]
    levels = level_halves(domains, 2 * subs)
    plan = {"levels": []}
    first = 0
    while first < len(levels):
        last = first + 1
        plan["levels"].append((first, last, span(owners_of(levels[first], domains), most_owners), span(levels[first], most)))
        first = last

    def kernel(*refs):
        step_kernel(domains, slots, subs, plan, own_index, *refs)

    return pl.pallas_call(
        kernel,
        out_shape=[jax.ShapeDtypeStruct((3, seg), jnp.float32)] * 2,
        in_specs=[ANYWHERE] * len(now) + [VMEM] * 3,
        out_specs=[VMEM] * 2,
        scratch_shapes=[
            pltpu.VMEM((domains, rows, seg), jnp.float32),
            pltpu.VMEM((2 * subs + 1, domains, ROWS, seg), jnp.float32),
            pltpu.VMEM((2 * subs, domains, ROWS, seg), jnp.float32),
            pltpu.VMEM((domains, ROWS, seg), jnp.float32),
            pltpu.VMEM((domains, 2, ROWS, LANES), jnp.float32),
            pltpu.SemaphoreType.DMA((domains,)),
        ],
        compiler_params=pltpu.CompilerParams(vmem_limit_bytes=STEP_VMEM * 2**20),
        cost_estimate=pl.CostEstimate(flops=10**7, bytes_accessed=6 * 10**7, transcendentals=10**6),
        name="step",
    )(*now, *weights)


def pack_kernel(*refs):
    here, block, held, sem = refs[:4], refs[4], refs[5:9], refs[9]
    copies = [pltpu.make_async_copy(src, dst, sem.at[n]) for n, (src, dst) in enumerate(zip(here, held))]
    for copy in copies:
        copy.start()
    for copy in copies:
        copy.wait()
    line_vectors, burgers, close_list, ghost_map = held
    slots, seg = close_list.shape
    block[:slots, :] = close_list[...].astype(jnp.float32)
    block[slots : slots + 3, :] = line_vectors[...]
    block[slots + 3 : slots + 6, :] = burgers[...]
    subs, wide = ghost_map.shape
    per = seg // wide
    for t in range(subs):
        at = slots + 6 + t // per
        block[at : at + 1, (t % per) * wide : (t % per + 1) * wide] = ghost_map[t : t + 1, :].astype(jnp.float32)


def packed(*arrays):
    slots, seg = arrays[2].shape
    return pl.pallas_call(
        pack_kernel,
        out_shape=jax.ShapeDtypeStruct((slots + 6 + arrays[3].size // seg, seg), jnp.float32),
        in_specs=[pl.BlockSpec(memory_space=pl.ANY)] * len(arrays),
        out_specs=VMEM,
        scratch_shapes=[pltpu.VMEM(a.shape, a.dtype) for a in arrays] + [pltpu.SemaphoreType.DMA((len(arrays),))],
        compiler_params=pltpu.CompilerParams(vmem_limit_bytes=PACK_VMEM * 2**20),
        name="pack",
    )(*arrays)


def split(rows):
    parts = []
    for _ in range(3):
        parts.append(rows.astype(jnp.bfloat16).astype(jnp.float32))
        rows = rows - parts[-1]
    return parts


SOURCE_PARTS = (0, 0, 1, 0, 2, 1)
TARGET_PARTS = (0, 1, 0, 2, 0, 1)
FEATURES = 48


def long_kernel(sources, seg, unroll, *refs):
    states, block = refs[: sources + 1], refs[sources + 1]
    out, held, features, aims, sem = refs[sources + 2 :]
    copy = pltpu.make_async_copy(block, held, sem)
    copy.start()
    cells = seg // LANES
    scale = 1.0 / math.sqrt((sources + 1) * LANES)
    zero = jnp.zeros((3, seg), jnp.float32)
    for s in range(sources + 1):
        vectors = (states[s][3:6, :], states[s][6:9, :])
        for n, vector in enumerate(vectors):
            parts = split(vector)
            for k, part in enumerate(SOURCE_PARTS):
                features[s, 18 * n + 3 * k : 18 * n + 3 * k + 3, :] = parts[part]
            if s == 0:
                for k, part in enumerate(TARGET_PARTS):
                    aims[18 * n + 3 * k : 18 * n + 3 * k + 3, :] = parts[part]
        for k, part in enumerate(split(states[s][0:3, :])):
            features[s, 36 + 3 * k : 39 + 3 * k, :] = part
        features[s, 45:48, :] = zero
    out[0:3, :] = states[0][0:3, :]
    out[3:4, :] = states[0][9:10, :]
    row = lax.broadcasted_iota(jnp.int32, (FEATURES, LANES), 0)
    column_of = [jnp.where((row >= 36) & (row < 45) & (row % 3 == c), 1.0, 0.0) for c in range(3)]

    def cell_at(lane):
        here = pl.ds(lane, LANES)
        aim = aims[:, here]
        right = jnp.concatenate([jnp.where(row < 18, aim, 0.0), jnp.where((row >= 18) & (row < 36), aim, 0.0), *column_of], 1).astype(jnp.bfloat16)
        mine = [states[0][c : c + 1, here] for c in range(3)]
        forces = [jnp.zeros((ROWS, LANES), jnp.float32)] * 3
        for s in range(sources + 1):
            left = jnp.transpose(features[s, :, here]).astype(jnp.bfloat16)
            made = jnp.dot(left, right, preferred_element_type=jnp.float32)
            line, burg, *at = [made[:, n * LANES : (n + 1) * LANES] for n in range(5)]
            delta = [m - a for m, a in zip(mine, at)]
            radius = delta[0] * delta[0] + delta[1] * delta[1] + delta[2] * delta[2] + long_core * long_core
            inverse = lax.rsqrt(radius)
            w = burg * line * (inverse * inverse * inverse)
            for c in range(3):
                forces[c] = forces[c] + jnp.sum((w * delta[c]).reshape(-1, ROWS, LANES), 0)
        return [jnp.sum(f, 0, keepdims=True) * scale for f in forces]

    def one(i, carry):
        lanes = [pl.multiple_of((i * unroll + u) * LANES, LANES) for u in range(unroll)]
        made = [cell_at(lane) for lane in lanes]
        for lane, forces in zip(lanes, made):
            for c in range(3):
                out[4 + c : 5 + c, pl.ds(lane, LANES)] = forces[c]
        return carry

    aims[36:48, :] = jnp.zeros((12, seg), jnp.float32)
    lax.fori_loop(0, cells // unroll, one, 0)
    copy.wait()


def long_range(state, others, block, unroll=8):
    seg = state.shape[1]
    return pl.pallas_call(
        lambda *refs: long_kernel(len(others), seg, unroll, *refs),
        out_shape=[jax.ShapeDtypeStruct((ROWS, seg), jnp.float32), jax.ShapeDtypeStruct(block.shape, block.dtype)],
        in_specs=[VMEM] * (1 + len(others)) + [pl.BlockSpec(memory_space=pl.ANY)],
        out_specs=[VMEM] * 2,
        scratch_shapes=[pltpu.VMEM((len(others) + 1, FEATURES, seg), jnp.float32), pltpu.VMEM((FEATURES, seg), jnp.float32), pltpu.SemaphoreType.DMA(())],
        compiler_params=pltpu.CompilerParams(vmem_limit_bytes=SMALL_VMEM * 2**20),
        cost_estimate=pl.CostEstimate(flops=10**7, bytes_accessed=2 * 10**7, transcendentals=10**6),
        name="long_range",
    )(state, *others, block)


def shifted(value, axis, steps):
    count = lax.axis_size(axis)
    return lax.ppermute(value, axis, [(i, (i + steps) % count) for i in range(count)])


def matched(value, axis, step):
    count = lax.axis_size(axis)
    return lax.ppermute(value, axis, [(i, i ^ step) for i in range(count)])


def cycle_neighbours(value, axis):
    count = lax.axis_size(axis)
    got = [matched(value, axis, 1), lax.ppermute(value, axis, [(i, (((i - 1) % count) ^ 1) + 1 if ((i - 1) % count) ^ 1 != count - 1 else 0) for i in range(count)])]
    for k in range(2, count // 4 + 1):
        got += [shifted(value, axis, k), shifted(value, axis, -k)]
    return got


def local(positions, line_vectors, burgers, mobility, close_list, ghost_map):
    slots, seg = close_list.shape
    subs = ghost_map.shape[0]
    half = lax.axis_size("dom") // 2
    own_index = lambda: lax.axis_index("dom")
    block = packed(line_vectors, burgers, close_list, ghost_map)
    state = jnp.concatenate([positions, line_vectors, burgers, mobility[None]], 0)
    others = cycle_neighbours(state, "blk")
    far_first = range(half - 1, 0, -1)
    blocks = [matched(block, "dom", 2 * j) for j in far_first[:3]]
    now, block = long_range(state, others, block)
    pair = jnp.concatenate([now, matched(now, "dom", 1)], 0)
    blocks, _ = lax.optimization_barrier((blocks, now))
    now = pair
    nows = [now] + [matched(now, "dom", 2 * j) for j in range(1, half)]
    blocks = [block] + blocks
    blocks = blocks + [matched(b, "dom", 1) for b in blocks]
    weights = pair_weights(blocks, slots, subs, own_index)
    nows, weights = lax.optimization_barrier((nows, weights))
    return tuple(step(nows, weights, subs, own_index))


def solution(mesh):
    spread = P(None, ("blk", "dom"))
    return jax.shard_map(
        local,
        mesh=mesh,
        in_specs=(spread, spread, spread, P(("blk", "dom")), spread, spread),
        out_specs=(spread, spread),
        check_vma=False,
    )
```

```python
import math

import jax
import jax.numpy as jnp
from jax import lax
from jax.experimental import pallas as pl
from jax.experimental.pallas import tpu as pltpu
from jax.sharding import PartitionSpec as P

LANES = 128
ROWS = 8
long_core = 1.0
short_core = 0.25
time_step = 0.05


def lane_gather(row_block, places):
    return jnp.take_along_axis(row_block, places, axis=1, mode="promise_in_bounds")


def level_halves(domains, evals):
    levels = [{(0, 0), (0, 1)}]
    for _ in range(evals - 1):
        last = levels[-1]
        grown = set(last)
        for domain in {d for d, _ in last}:
            grown.add(((domain - 1) % domains, 1))
            grown.add(((domain + 1) % domains, 0))
        levels.append(grown)
    return [sorted(level) for level in levels[::-1]]


EXPAND = 4
SMALL_VMEM = 8
PACK_VMEM = 60
WEIGHT_VMEM = 24
STEP_VMEM = 24

def far_first(half):
    return [*range(half // 2, half), *range(1, half // 2)]


def fetch(refs, held, me, sem, order):
    half = held.shape[0] // 2
    copies = []
    for j in range(half):
        for other in range(2):
            at = other * half + j
            src = refs[at] if len(refs) > half else refs[j].at[pl.ds(other * held.shape[1], held.shape[1])]
            place = lax.rem((me ^ (2 * order[j] + other)) - me + 2 * half, 2 * half)
            copies.append(pltpu.make_async_copy(src, held.at[place], sem.at[at]))
    for copy in copies:
        copy.start()
    for copy in copies:
        copy.wait()


def weights_kernel(domains, slots, subs, plan, own_index, *refs):
    block_refs = refs[:domains]
    weight, close, gplaces, pack, still_rows, still, sem = refs[domains:]
    seg = pack.shape[2]
    cells = seg // LANES
    groups = slots // ROWS
    half_cells = cells // 2
    half_lanes = half_cells * LANES
    ghosts = seg // (2 * (subs // 2))
    me = own_index()
    scale = 1.0 / math.sqrt(slots)
    LINE, BURG, GHOST = slots, slots + 3, slots + 6
    fetch(block_refs, pack, me, sem, [0, *far_first(domains // 2)])

    row = lax.broadcasted_iota(jnp.int32, (ROWS, LANES), 0)
    x_rows = row < 2
    y_rows = row < 4

    even_row = lax.rem(row, 2) == 0

    def bcast(ref, index, at, lane):
        return jnp.broadcast_to(ref[*index, at : at + 1, pl.ds(lane, LANES)], (ROWS, LANES))

    def spread(ref, d, at, lane):
        x, y, z = (bcast(ref, (d,), at + c, lane) for c in range(3))
        return jnp.where(x_rows, x, jnp.where(y_rows, y, z))

    def expand(d, carry):
        for q in range(cells):
            here = pl.ds(q * LANES, LANES)
            for at, slot in ((LINE, 0), (BURG, 1)):
                still_rows[slot, d, :, here] = spread(pack, d, at, q * LANES)
        for sub in range(subs):
            for side in range(2):
                lane = (sub % 2) * 2 * ghosts + side * ghosts
                at = GHOST + sub // 2
                place = jnp.where(even_row, bcast(pack, (d,), at, lane), bcast(pack, (d,), at, lane + LANES))
                gplaces[d, :, pl.ds((2 * sub + side) * LANES, LANES)] = place.astype(jnp.int32)
        return carry

    lax.fori_loop(0, domains, expand, 0, unroll=EXPAND)

    def owner_picks(owners, sub, sources):
        made = []
        for offset, _ in owners:
            d = offset
            for side in range(2):
                place = gplaces[d, :, pl.ds(pl.multiple_of((2 * sub + side) * LANES, LANES), LANES)]
                lane = place & (LANES - 1)
                cell = place >> 7
                to = (d + (1 if side else domains - 1)) % domains
                for source, ref, slot in sources:
                    out = None
                    for k in range(half_cells):
                        got = lane_gather(source[d, :, pl.ds(side * half_lanes + k * LANES, LANES)], lane)
                        out = got if out is None else jnp.where(cell == side * half_cells + k, got, out)
                    made.append((ref, slot, to, 1 - side, out))
        for ref, slot, to, at, out in made:
            ref[*slot, to, at] = out

    def over(span, body):
        steps, count, entries = span
        if steps == 1:
            body(entries)
            return
        def one(i, carry):
            body([tuple(chosen(i, [entries[n * count + u][at] for n in range(steps)]) for at in (0, 1)) for u in range(count)])
            return carry
        lax.fori_loop(0, steps, one, 0)

    def items(entries):
        for offset, side in entries:
            d = offset
            for k in range(half_cells):
                lane = side * half_lanes + k * LANES
                yield d, lane if isinstance(lane, int) else pl.multiple_of(lane, LANES), k

    def dots(mine, theirs):
        return mine[0] * theirs[0] + mine[1] * theirs[1] + mine[2] * theirs[2]

    def pair_weight(mine, source, places):
        theirs = [lane_gather(m, places) for m in source]
        return dots(mine[:3], theirs[:3]) * dots(mine[3:], theirs[3:]) * scale

    def ghost_rows(ref, slot, d, k):
        side, pair = divmod(k, 2)
        return [bcast(ref, (*slot, d, side), 2 * c + pair, 0) for c in range(3)]

    def blocks(d, lane):
        for g in range(groups):
            yield (d, slice(g * ROWS, (g + 1) * ROWS), pl.ds(lane, LANES))

    def weights(entries, upto):
        made = []
        for d, lane, k in items(entries):
            mine = [bcast(pack, (d,), LINE + c, lane) for c in range(6)]
            far = [ghost_rows(still, (sub, 0), d, k) + ghost_rows(still, (sub, 1), d, k) for sub in range(upto)]
            for at in blocks(d, lane):
                entry = pack[at].astype(jnp.int32)
                places = entry & (LANES - 1)
                near, held = entry < LANES, entry < 2 * LANES
                near_w = pair_weight(mine, mine, places)
                made.append((close.at[at], entry))
                for sub in range(upto):
                    made.append((weight.at[(sub, *at)], jnp.where(near, near_w, jnp.where(held, pair_weight(mine, far[sub], places), 0.0))))
        for ref, value in made:
            ref[...] = value

    for sub in range(subs):
        over(plan["still"][sub], lambda owners: owner_picks(owners, sub, ((still_rows.at[0], still, (sub, 0)), (still_rows.at[1], still, (sub, 1)))))
    for upto, span in plan["weights"]:
        over(span, lambda entries: weights(entries, upto))


def step_kernel(domains, slots, subs, plan, own_index, *refs):
    half = domains // 2
    now_refs = refs[:half]
    weight, close, gplaces = refs[half : half + 3]
    out_pos, out_vel = refs[half + 3 : half + 5]
    now, state, vels, long_, ghost, sem = refs[half + 5 :]
    seg = now.shape[2]
    evals = vels.shape[0]
    cells = seg // LANES
    groups = slots // ROWS
    half_cells = cells // 2
    half_lanes = half_cells * LANES
    me = own_index()
    POS, MOB, FAR = 0, 3, 4
    fetch(now_refs, now, me, sem, range(domains // 2))

    row = lax.broadcasted_iota(jnp.int32, (ROWS, LANES), 0)
    x_rows = row < 2
    y_rows = row < 4

    def bcast(ref, index, at, lane):
        return jnp.broadcast_to(ref[*index, at : at + 1, pl.ds(lane, LANES)], (ROWS, LANES))

    def spread(d, at, lane):
        x, y, z = (bcast(now, (d,), at + c, lane) for c in range(3))
        return jnp.where(x_rows, x, jnp.where(y_rows, y, z))

    def expand(d, carry):
        for q in range(cells):
            here = pl.ds(q * LANES, LANES)
            state[0, d, :, here] = spread(d, POS, q * LANES)
            long_[d, :, here] = spread(d, FAR, q * LANES)
        return carry

    lax.fori_loop(0, domains, expand, 0, unroll=EXPAND)

    def owner_picks(owners, sub, sources):
        made = []
        for offset, _ in owners:
            d = offset
            for side in range(2):
                place = gplaces[d, :, pl.ds(pl.multiple_of((2 * sub + side) * LANES, LANES), LANES)]
                lane = place & (LANES - 1)
                cell = place >> 7
                to = (d + (1 if side else domains - 1)) % domains
                for source, ref, slot in sources:
                    out = None
                    for k in range(half_cells):
                        got = lane_gather(source[d, :, pl.ds(side * half_lanes + k * LANES, LANES)], lane)
                        out = got if out is None else jnp.where(cell == side * half_cells + k, got, out)
                    made.append((ref, slot, to, 1 - side, out))
        for ref, slot, to, at, out in made:
            ref[*slot, to, at] = out

    def over(span, body):
        steps, count, entries = span
        if steps == 1:
            body(entries)
            return
        def one(i, carry):
            body([tuple(chosen(i, [entries[n * count + u][at] for n in range(steps)]) for at in (0, 1)) for u in range(count)])
            return carry
        lax.fori_loop(0, steps, one, 0)

    def items(entries):
        for offset, side in entries:
            d = offset
            for k in range(half_cells):
                lane = side * half_lanes + k * LANES
                yield d, lane if isinstance(lane, int) else pl.multiple_of(lane, LANES), k

    def ghost_rows(ref, slot, d, k):
        side, pair = divmod(k, 2)
        return [bcast(ref, (*slot, d, side), 2 * c + pair, 0) for c in range(3)]

    def blocks(d, lane):
        for g in range(groups):
            yield (d, slice(g * ROWS, (g + 1) * ROWS), pl.ds(lane, LANES))

    def total(block):
        for shift in (4, 2, 1):
            block = block + pltpu.roll(block, shift, 0)
        return block

    def force(level, sub, d, lane, k):
        mine = [bcast(state, (level, d), 2 * c, lane) for c in range(3)]
        far = ghost_rows(ghost, (), d, k)
        sums = [None] * 3
        for at in blocks(d, lane):
            entry = close[at]
            places = entry & (LANES - 1)
            near = entry < LANES
            delta = [m - jnp.where(near, lane_gather(m, places), lane_gather(f, places)) for m, f in zip(mine, far)]
            radius = delta[0] * delta[0] + delta[1] * delta[1] + delta[2] * delta[2] + short_core * short_core
            inverse = lax.rsqrt(radius)
            w = weight[(sub, *at)] * (inverse * inverse * inverse)
            for c in range(3):
                term = w * delta[c]
                sums[c] = term if sums[c] is None else sums[c] + term
        sums = [total(s) for s in sums]
        return jnp.where(x_rows, sums[0], jnp.where(y_rows, sums[1], sums[2]))

    def evaluate(level, owners, halves):
        sub = level // 2
        stage = level % 2
        base = level - stage
        over(owners, lambda owners: owner_picks(owners, sub, ((state.at[level], ghost, ()),)))

        def one(entries):
            made = []
            for d, lane, k in items(entries):
                here = pl.ds(lane, LANES)
                vel = bcast(now, (d,), MOB, lane) * (long_[d, :, here] + force(level, sub, d, lane, k))
                if stage == 1:
                    vel = 0.5 * (vels[base, d, :, here] + vel)
                made.append((d, here, vel, state[base, d, :, here] + time_step * vel))
            for d, here, vel, moved in made:
                vels[level, d, :, here] = vel
                state[level + 1, d, :, here] = moved

        over(halves, one)

    for first, last, owners, halves in plan["levels"]:
        if last - first == 1:
            evaluate(first, owners, halves)
        else:
            lax.fori_loop(first, last, lambda level, carry: (evaluate(level, owners, halves), carry)[1], 0)

    for c in range(3):
        out_pos[c : c + 1, :] = state[evals, 0, 2 * c : 2 * c + 1, :]
        out_vel[c : c + 1, :] = vels[evals - 1, 0, 2 * c : 2 * c + 1, :]


def span(entries, limit):
    count = min(range(1, limit + 1), key=lambda c: (-(-len(entries) // c) * (c + 0.5), c))
    steps = -(-len(entries) // count)
    return steps, count, entries + [entries[-1]] * (steps * count - len(entries))


def chosen(step, values):
    if len(set(values)) == 1:
        return values[0]
    if [v - values[0] for v in values] == [n * (values[1] - values[0]) for n in range(len(values))]:
        return values[0] + step * (values[1] - values[0])
    out = values[-1]
    for n in range(len(values) - 2, -1, -1):
        out = jnp.where(step == n, values[n], out)
    return out


def owners_of(level, domains):
    return sorted({((d + s) % domains, 0) for d, _ in level for s in (1, -1)})


ANYWHERE = pl.BlockSpec(memory_space=pl.ANY)
VMEM = pl.BlockSpec(memory_space=pltpu.VMEM)


def pair_weights(blocks, slots, subs, own_index, most=6, most_owners=8):
    domains = len(blocks)
    rows, seg = blocks[0].shape
    levels = level_halves(domains, 2 * subs)
    plan = {"still": [span(owners_of(levels[2 * t], domains), most_owners) for t in range(subs)], "weights": []}
    for upto in range(1, subs + 1):
        after = levels[2 * upto] if upto < subs else []
        only = [h for h in levels[2 * upto - 2] if h not in after]
        if only:
            plan["weights"].append((upto, span(only, most)))

    def kernel(*refs):
        weights_kernel(domains, slots, subs, plan, own_index, *refs)

    return pl.pallas_call(
        kernel,
        out_shape=[
            jax.ShapeDtypeStruct((subs, domains, slots, seg), jnp.float32),
            jax.ShapeDtypeStruct((domains, slots, seg), jnp.int32),
            jax.ShapeDtypeStruct((domains, ROWS, seg), jnp.int32),
        ],
        in_specs=[ANYWHERE] * domains,
        out_specs=[VMEM] * 3,
        scratch_shapes=[
            pltpu.VMEM((domains, rows, seg), jnp.float32),
            pltpu.VMEM((2, domains, ROWS, seg), jnp.float32),
            pltpu.VMEM((subs, 2, domains, 2, ROWS, LANES), jnp.float32),
            pltpu.SemaphoreType.DMA((domains,)),
        ],
        compiler_params=pltpu.CompilerParams(vmem_limit_bytes=WEIGHT_VMEM * 2**20),
        cost_estimate=pl.CostEstimate(flops=10**7, bytes_accessed=4 * 10**7, transcendentals=0),
        name="weights",
    )(*blocks)


def step(now, weights, subs, own_index, most=16, most_owners=8):
    domains = 2 * len(now)
    rows, seg = now[0].shape[0] // 2, now[0].shape[1]
    slots = weights[0].shape[2]
    levels = level_halves(domains, 2 * subs)
    plan = {"levels": []}
    first = 0
    while first < len(levels):
        last = first + 1
        plan["levels"].append((first, last, span(owners_of(levels[first], domains), most_owners), span(levels[first], most)))
        first = last

    def kernel(*refs):
        step_kernel(domains, slots, subs, plan, own_index, *refs)

    return pl.pallas_call(
        kernel,
        out_shape=[jax.ShapeDtypeStruct((3, seg), jnp.float32)] * 2,
        in_specs=[ANYWHERE] * len(now) + [VMEM] * 3,
        out_specs=[VMEM] * 2,
        scratch_shapes=[
            pltpu.VMEM((domains, rows, seg), jnp.float32),
            pltpu.VMEM((2 * subs + 1, domains, ROWS, seg), jnp.float32),
            pltpu.VMEM((2 * subs, domains, ROWS, seg), jnp.float32),
            pltpu.VMEM((domains, ROWS, seg), jnp.float32),
            pltpu.VMEM((domains, 2, ROWS, LANES), jnp.float32),
            pltpu.SemaphoreType.DMA((domains,)),
        ],
        compiler_params=pltpu.CompilerParams(vmem_limit_bytes=STEP_VMEM * 2**20),
        cost_estimate=pl.CostEstimate(flops=10**7, bytes_accessed=6 * 10**7, transcendentals=10**6),
        name="step",
    )(*now, *weights)


def pack_kernel(*refs):
    here, block, held, sem = refs[:4], refs[4], refs[5:9], refs[9]
    copies = [pltpu.make_async_copy(src, dst, sem.at[n]) for n, (src, dst) in enumerate(zip(here, held))]
    for copy in copies:
        copy.start()
    for copy in copies:
        copy.wait()
    line_vectors, burgers, close_list, ghost_map = held
    slots, seg = close_list.shape
    block[:slots, :] = close_list[...].astype(jnp.float32)
    block[slots : slots + 3, :] = line_vectors[...]
    block[slots + 3 : slots + 6, :] = burgers[...]
    subs, wide = ghost_map.shape
    per = seg // wide
    for t in range(subs):
        at = slots + 6 + t // per
        block[at : at + 1, (t % per) * wide : (t % per + 1) * wide] = ghost_map[t : t + 1, :].astype(jnp.float32)


def packed(*arrays):
    slots, seg = arrays[2].shape
    return pl.pallas_call(
        pack_kernel,
        out_shape=jax.ShapeDtypeStruct((slots + 6 + arrays[3].size // seg, seg), jnp.float32),
        in_specs=[pl.BlockSpec(memory_space=pl.ANY)] * len(arrays),
        out_specs=VMEM,
        scratch_shapes=[pltpu.VMEM(a.shape, a.dtype) for a in arrays] + [pltpu.SemaphoreType.DMA((len(arrays),))],
        compiler_params=pltpu.CompilerParams(vmem_limit_bytes=PACK_VMEM * 2**20),
        name="pack",
    )(*arrays)


def split(rows):
    parts = []
    for _ in range(3):
        parts.append(rows.astype(jnp.bfloat16).astype(jnp.float32))
        rows = rows - parts[-1]
    return parts


SOURCE_PARTS = (0, 0, 1, 0, 2, 1)
TARGET_PARTS = (0, 1, 0, 2, 0, 1)
FEATURES = 48


def long_kernel(sources, seg, unroll, *refs):
    states, block = refs[: sources + 1], refs[sources + 1]
    out, held, features, aims, sem = refs[sources + 2 :]
    copy = pltpu.make_async_copy(block, held, sem)
    copy.start()
    cells = seg // LANES
    scale = 1.0 / math.sqrt((sources + 1) * LANES)
    zero = jnp.zeros((3, seg), jnp.float32)
    for s in range(sources + 1):
        vectors = (states[s][3:6, :], states[s][6:9, :])
        for n, vector in enumerate(vectors):
            parts = split(vector)
            for k, part in enumerate(SOURCE_PARTS):
                features[s, 18 * n + 3 * k : 18 * n + 3 * k + 3, :] = parts[part]
            if s == 0:
                for k, part in enumerate(TARGET_PARTS):
                    aims[18 * n + 3 * k : 18 * n + 3 * k + 3, :] = parts[part]
        for k, part in enumerate(split(states[s][0:3, :])):
            features[s, 36 + 3 * k : 39 + 3 * k, :] = part
        features[s, 45:48, :] = zero
    out[0:3, :] = states[0][0:3, :]
    out[3:4, :] = states[0][9:10, :]
    row = lax.broadcasted_iota(jnp.int32, (FEATURES, LANES), 0)
    column_of = [jnp.where((row >= 36) & (row < 45) & (row % 3 == c), 1.0, 0.0) for c in range(3)]

    def cell_at(lane):
        here = pl.ds(lane, LANES)
        aim = aims[:, here]
        right = jnp.concatenate([jnp.where(row < 18, aim, 0.0), jnp.where((row >= 18) & (row < 36), aim, 0.0), *column_of], 1).astype(jnp.bfloat16)
        mine = [states[0][c : c + 1, here] for c in range(3)]
        forces = [jnp.zeros((ROWS, LANES), jnp.float32)] * 3
        for s in range(sources + 1):
            left = jnp.transpose(features[s, :, here]).astype(jnp.bfloat16)
            made = jnp.dot(left, right, preferred_element_type=jnp.float32)
            line, burg, *at = [made[:, n * LANES : (n + 1) * LANES] for n in range(5)]
            delta = [m - a for m, a in zip(mine, at)]
            radius = delta[0] * delta[0] + delta[1] * delta[1] + delta[2] * delta[2] + long_core * long_core
            inverse = lax.rsqrt(radius)
            w = burg * line * (inverse * inverse * inverse)
            for c in range(3):
                forces[c] = forces[c] + jnp.sum((w * delta[c]).reshape(-1, ROWS, LANES), 0)
        return [jnp.sum(f, 0, keepdims=True) * scale for f in forces]

    def one(i, carry):
        lanes = [pl.multiple_of((i * unroll + u) * LANES, LANES) for u in range(unroll)]
        made = [cell_at(lane) for lane in lanes]
        for lane, forces in zip(lanes, made):
            for c in range(3):
                out[4 + c : 5 + c, pl.ds(lane, LANES)] = forces[c]
        return carry

    aims[36:48, :] = jnp.zeros((12, seg), jnp.float32)
    lax.fori_loop(0, cells // unroll, one, 0)
    copy.wait()


def long_range(state, others, block, unroll=8):
    seg = state.shape[1]
    return pl.pallas_call(
        lambda *refs: long_kernel(len(others), seg, unroll, *refs),
        out_shape=[jax.ShapeDtypeStruct((ROWS, seg), jnp.float32), jax.ShapeDtypeStruct(block.shape, block.dtype)],
        in_specs=[VMEM] * (1 + len(others)) + [pl.BlockSpec(memory_space=pl.ANY)],
        out_specs=[VMEM] * 2,
        scratch_shapes=[pltpu.VMEM((len(others) + 1, FEATURES, seg), jnp.float32), pltpu.VMEM((FEATURES, seg), jnp.float32), pltpu.SemaphoreType.DMA(())],
        compiler_params=pltpu.CompilerParams(vmem_limit_bytes=SMALL_VMEM * 2**20),
        cost_estimate=pl.CostEstimate(flops=10**7, bytes_accessed=2 * 10**7, transcendentals=10**6),
        name="long_range",
    )(state, *others, block)


def shifted(value, axis, steps):
    count = lax.axis_size(axis)
    return lax.ppermute(value, axis, [(i, (i + steps) % count) for i in range(count)])


def matched(value, axis, step):
    count = lax.axis_size(axis)
    return lax.ppermute(value, axis, [(i, i ^ step) for i in range(count)])


def cycle_neighbours(value, axis):
    count = lax.axis_size(axis)
    got = [matched(value, axis, 1), lax.ppermute(value, axis, [(i, (((i - 1) % count) ^ 1) + 1 if ((i - 1) % count) ^ 1 != count - 1 else 0) for i in range(count)])]
    for k in range(2, count // 4 + 1):
        got += [shifted(value, axis, k), shifted(value, axis, -k)]
    return got


def local(positions, line_vectors, burgers, mobility, close_list, ghost_map):
    slots, seg = close_list.shape
    subs = ghost_map.shape[0]
    half = lax.axis_size("dom") // 2
    own_index = lambda: lax.axis_index("dom")
    block = packed(line_vectors, burgers, close_list, ghost_map)
    state = jnp.concatenate([positions, line_vectors, burgers, mobility[None]], 0)
    others = cycle_neighbours(state, "blk")
    blocks = [matched(block, "dom", 2 * j) for j in far_first(half)]
    now, block = long_range(state, others, block)
    pair = jnp.concatenate([now, matched(now, "dom", 1)], 0)
    blocks, _ = lax.optimization_barrier((blocks, now))
    now = pair
    nows = [now] + [matched(now, "dom", 2 * j) for j in range(1, half)]
    blocks = [block] + blocks
    blocks = blocks + [matched(b, "dom", 1) for b in blocks]
    weights = pair_weights(blocks, slots, subs, own_index)
    nows, weights = lax.optimization_barrier((nows, weights))
    return tuple(step(nows, weights, subs, own_index))


def solution(mesh):
    spread = P(None, ("blk", "dom"))
    return jax.shard_map(
        local,
        mesh=mesh,
        in_specs=(spread, spread, spread, P(("blk", "dom")), spread, spread),
        out_specs=(spread, spread),
        check_vma=False,
    )
```
